32 devices in a mesh: grp: 2 (over y), blk: 4 (over z), sub: 2 (over x), lev: 2 (over core).
Axes of the slice: x: 2, y: 2, z: 4, core: 2. Of those that a mesh axis runs over, the one named last changes fastest.
Arguments:
- tracers: float32 [4, 20, 32, 16, 128], P('grp', 'lev', ('blk', 'sub')), parts along dimension 0, may hold values from -6 to 6
- horizontal_diffusivity: float32 [32, 16, 128], P(('blk', 'sub')), may hold values from 0.03 to 0.12
- vertical_mixing: float32 [19], replicated, may hold values from 0.02 to 0.2
- layer_thickness: float32 [20], replicated, may hold values from 0.1 to 0.4
- surface_diagonal: float32 [32, 16, 128], P(('blk', 'sub')), may hold values from 0.3 to 3
- neighbours: int32 [32, 4], P(('blk', 'sub')), may hold values from -1 to 31, as said below
- baro_blocks: int32 [48], P(('blk', 'sub', 'lev')), may hold values from -1 to 31, as said below
Outputs:
- tracer_next: float32 [4, 20, 32, 16, 128], P('grp', 'lev', ('blk', 'sub')), parts along dimension 0
- pressure: float32 [40, 32, 16, 128], P(('grp', 'lev'), ('blk', 'sub')), parts along dimension 0
- surface_height: float32 [96, 16, 128], P(('grp', 'blk', 'sub', 'lev')), parts along dimension 0
The draws below stay inside these ranges and needn't reach their ends.
There are 2 independent parts, one for each index of `grp`. The reference program is written for one: setup_inputs(seed, part) draws one part's arguments, and reference() takes and returns one part's arrays. A program takes and returns all parts, laid end to end along the dimension named above; an argument that names none is the same for every part. Nothing has to cross between parts.
Inputs may be any that keep to these rules, and one draw needn't show every extreme that they name: Blocks lie on a grid of 12 x 4 block places of which a third are land; ocean blocks are ranked in order along a curve that runs along each block row, alternately left to right and right to left. neighbours[q, s] is the rank of the ocean block beside q on side s (0 previous row, 1 next row, 2 previous column, 3 next column), or -1 for land or the grid's edge; the relation is symmetric, and a neighbour's rank lies in the same or an adjacent run of 8 ranks starting at a multiple of 8. `baro_blocks`: each surface owner (in the order blk, sub, lev) holds a run of consecutive ranks in its first slots and -1 in the rest; the runs follow one another and cover all ranks, those of one blk index b covering ranks 8 * b to 8 * b + 7. In each blk index one owner holds 3 ranks, one owner beside it within that index holds a quarter of 4, and all others half of 4.
All inputs are finite; a program needn't handle non-finite values.
Results may differ from the reference program's by a relative error of at most 0.0001.
Values sent between devices are 32-bit elements; how exact they have to be, the bound alone decides.
A program may use at most 64 MiB of HBM per device.

```python
import math
import jax
import jax.numpy as jnp
from jax import lax

BY = 16
BX = 128
LEVELS = 20
ITERS = 3
NBD = 4
GROUP = 8
NR = 32
BGX = 4
BGY = 12
GROUPS = 4
PEERS = 4
CAP = 3
SLOTS = 48


def draw_tracers(key, part):
    key = jax.random.fold_in(key, 3)
    ranks = jnp.arange(NR, dtype=jnp.float32) / (NR - 1)
    shape = (2, LEVELS, NR, BY, BX)
    noise = jnp.clip(jax.random.normal(key, shape, jnp.float32), -4.0, 4.0)
    return noise * (0.5 + ranks)[None, None, :, None, None]


def draw_neighbours(key, part):
    key = jax.random.fold_in(key, 5)
    total = BGY * BGX
    order = jax.random.permutation(key, total)
    wet_grid = (order >= total - NR).reshape(BGY, BGX)
    row_index = jnp.arange(BGY, dtype=jnp.int32)[:, None]
    col_index = jnp.arange(BGX, dtype=jnp.int32)[None, :]
    curve_col = jnp.where(row_index % 2 == 0, col_index, BGX - 1 - col_index)
    curve_pos = row_index * BGX + curve_col
    wet_curve = jnp.zeros((total,), jnp.int32).at[curve_pos.reshape(-1)].set(wet_grid.reshape(-1).astype(jnp.int32))
    rank_curve = jnp.cumsum(wet_curve) - 1
    rank_grid = jnp.where(wet_grid, rank_curve[curve_pos], -1)
    padded = jnp.pad(rank_grid, 1, constant_values=-1)
    sides = jnp.stack([padded[:-2, 1:-1], padded[2:, 1:-1], padded[1:-1, :-2], padded[1:-1, 2:]], axis=-1)
    target = jnp.where(wet_grid, rank_grid, NR)
    return jnp.full((NR, 4), -1, jnp.int32).at[target].set(sides, mode='drop')


def draw_baro_blocks(key, part):
    key = jax.random.fold_in(key, 7)
    half_count = NBD // 2
    quarter = NBD // 4
    heavy = jax.random.randint(key, (GROUPS, 1), 0, PEERS)
    partner = jnp.where(heavy < PEERS - 1, heavy + 1, heavy - 1)
    owner_ids = jnp.arange(PEERS, dtype=jnp.int32)[None, :]
    counts = half_count + quarter * (owner_ids == heavy).astype(jnp.int32) - quarter * (owner_ids == partner).astype(jnp.int32)
    group_base = jnp.arange(GROUPS, dtype=jnp.int32)[:, None] * GROUP
    starts = jnp.cumsum(counts, axis=1) - counts + group_base
    slot_ids = jnp.arange(CAP, dtype=jnp.int32)[None, None, :]
    ranks = jnp.where(slot_ids < counts[:, :, None], starts[:, :, None] + slot_ids, -1)
    return ranks.reshape(SLOTS)


def block_scale(own_key, dims, cuts, low, high):
    factor_of, own = 1.0, jax.random.fold_in(own_key, 6)
    for axis_at, shards_of in cuts:
        draws = jnp.exp(jax.random.uniform(jax.random.fold_in(own, axis_at), (shards_of,), jnp.float32, low / len(cuts), high / len(cuts)))
        factor_of = factor_of * jnp.repeat(draws, dims[axis_at] // shards_of).reshape([-1 if axis == axis_at else 1 for axis in range(len(dims))])
    return factor_of


def setup_inputs(seed: int = 0, part: int = 0) -> dict:
    seeds = jax.random.split(jax.random.key(seed), 8)
    part_splits = jax.random.split(jax.random.fold_in(seeds[7], part), 8)
    tracers = draw_tracers(jax.random.fold_in(jax.random.fold_in(seeds[7], part), 71), part)
    horizontal_diffusivity = jnp.clip(jnp.exp(math.log(0.12) - 1.3862944 * jax.random.uniform(seeds[1], (NR, BY, BX), jnp.float32) ** block_scale(seeds[1], (NR, BY, BX), ((0, 8),), -0.2, 0.2)), 0.03, 0.12)
    vertical_mixing = jnp.clip(jnp.exp(jax.random.uniform(seeds[2], (LEVELS - 1,), jnp.float32, math.log(0.02), math.log(0.2))), 0.02, 0.2)
    layer_thickness = jnp.clip(jnp.exp(jax.random.uniform(seeds[3], (LEVELS,), jnp.float32, math.log(0.1), math.log(0.4))), 0.1, 0.4)
    surface_diagonal = jnp.clip(jnp.exp(math.log(3.0) - 2.3025851 * jax.random.uniform(seeds[4], (NR, BY, BX), jnp.float32) ** block_scale(seeds[4], (NR, BY, BX), ((0, 8),), -0.2, 0.2)), 0.3, 3.0)
    neighbours = draw_neighbours(jax.random.fold_in(seeds[7], 71), part)
    baro_blocks = draw_baro_blocks(jax.random.fold_in(seeds[7], 71), part)
    return dict(tracers=tracers, horizontal_diffusivity=horizontal_diffusivity, vertical_mixing=vertical_mixing, layer_thickness=layer_thickness, surface_diagonal=surface_diagonal, neighbours=neighbours, baro_blocks=baro_blocks)


def edge_strips(values):
    return jnp.concatenate([values[..., 0, :], values[..., -1, :], values[..., :, 0], values[..., :, -1]], axis=-1)


def pick_halos(gathered, row_count, col_count):
    halo_above = gathered[..., 0, col_count:2 * col_count]
    halo_below = gathered[..., 1, 0:col_count]
    halo_west = gathered[..., 2, 2 * col_count + row_count:2 * col_count + 2 * row_count]
    halo_east = gathered[..., 3, 2 * col_count:2 * col_count + row_count]
    return halo_above, halo_below, halo_west, halo_east


def spread_sum(values, halos, opened):
    row_count, col_count = values.shape[-2], values.shape[-1]
    halo_above, halo_below, halo_west, halo_east = halos
    from_above = jnp.concatenate([halo_above[..., None, :], values[..., :-1, :]], axis=-2)
    from_below = jnp.concatenate([values[..., 1:, :], halo_below[..., None, :]], axis=-2)
    from_west = jnp.concatenate([halo_west[..., :, None], values[..., :, :-1]], axis=-1)
    from_east = jnp.concatenate([values[..., :, 1:], halo_east[..., :, None]], axis=-1)
    row_ids = lax.broadcasted_iota(jnp.int32, (row_count, col_count), 0)
    col_ids = lax.broadcasted_iota(jnp.int32, (row_count, col_count), 1)
    unity = jnp.ones((row_count, col_count), jnp.float32)
    open_up = jnp.where(row_ids == 0, opened[:, 0, None, None], unity)
    open_down = jnp.where(row_ids == row_count - 1, opened[:, 1, None, None], unity)
    open_west = jnp.where(col_ids == 0, opened[:, 2, None, None], unity)
    open_east = jnp.where(col_ids == col_count - 1, opened[:, 3, None, None], unity)
    return open_up * (from_above - values) + open_down * (from_below - values) + open_west * (from_west - values) + open_east * (from_east - values)


def reference(tracers, horizontal_diffusivity, vertical_mixing, layer_thickness, surface_diagonal, neighbours, baro_blocks):
    level_count = tracers.shape[1]
    row_count, col_count = tracers.shape[3], tracers.shape[4]
    opened = (neighbours >= 0).astype(jnp.float32)
    clipped = jnp.maximum(neighbours, 0)
    boundary_zero = jnp.zeros((1,), jnp.float32)
    mixing_pad = jnp.concatenate([boundary_zero, vertical_mixing, boundary_zero])

    def level_update(level):
        current = lax.dynamic_index_in_dim(tracers, level, 1, keepdims=False)
        shallower = lax.dynamic_index_in_dim(tracers, jnp.maximum(level - 1, 0), 1, keepdims=False)
        deeper = lax.dynamic_index_in_dim(tracers, jnp.minimum(level + 1, level_count - 1), 1, keepdims=False)
        rate_above = mixing_pad[level]
        rate_below = mixing_pad[level + 1]
        vertical = rate_below * (deeper - current) - rate_above * (current - shallower)
        gathered = jnp.take(edge_strips(current), clipped, axis=1)
        spread = spread_sum(current, pick_halos(gathered, row_count, col_count), opened)
        stepped = current + horizontal_diffusivity * spread + vertical
        buoyancy = 0.6 * stepped[0] + 0.05 * stepped[0] * stepped[0] - 0.8 * stepped[1]
        return stepped, layer_thickness[level] * buoyancy

    stepped_all, weighted = lax.map(level_update, jnp.arange(level_count, dtype=jnp.int32))
    tracer_next = jnp.transpose(stepped_all, (1, 0, 2, 3, 4))
    column = jnp.cumsum(weighted, axis=0)
    forcing = column[-1]

    def operate(values):
        gathered = jnp.take(edge_strips(values), clipped, axis=0)
        return surface_diagonal * values - spread_sum(values, pick_halos(gathered, row_count, col_count), opened)

    solution = jnp.zeros_like(forcing)
    residual = forcing
    direction = forcing
    norm_now = jnp.sum(residual * residual)
    for iteration in range(ITERS):
        applied = operate(direction)
        step_size = norm_now / jnp.sum(direction * applied)
        solution = solution + step_size * direction
        residual = residual - step_size * applied
        norm_next = jnp.sum(residual * residual)
        direction = residual + (norm_next / norm_now) * direction
        norm_now = norm_next
    pressure = solution[None] - column
    occupied = baro_blocks >= 0
    surface_height = jnp.where(occupied[:, None, None], jnp.take(solution, jnp.maximum(baro_blocks, 0), axis=0), 0.0)
    return tracer_next, pressure, surface_height
```

```python
import functools

import jax
import jax.numpy as jnp
from jax import lax
from jax.experimental import pallas as pl
from jax.experimental.pallas import tpu as pltpu
from jax.sharding import PartitionSpec as P

ITERS = 3
F32 = jnp.float32
HIGH = lax.Precision.HIGHEST


def five_point(v, before, after, up, down, west, east, q, row, lane):
    rows, cols = v.shape
    xw = jnp.where(lane == cols - 1, jnp.where(west == q - 1, before, after), v)
    xe = jnp.where(lane == 0, jnp.where(east == q - 1, before, after), v)
    dw = jnp.where((lane == 0) & (west < 0), 0.0, pltpu.roll(xw, 1, 1) - v)
    de = jnp.where((lane == cols - 1) & (east < 0), 0.0, pltpu.roll(xe, cols - 1, 1) - v)
    fa = jnp.where(row == 0, jnp.broadcast_to(up, v.shape), pltpu.roll(v, 1, 0))
    fb = jnp.where(row == rows - 1, jnp.broadcast_to(down, v.shape), pltpu.roll(v, rows - 1, 0))
    return (fa - v) + (fb - v) + dw + de


def kernel(
    B, S, ITEMS,
    tr, hd, vm, lt, sd, nb, baro,
    out_tr, out_p, out_s,
    X, Y, C, TOPS, BOTS, HA, HB, CP, CR, TOT, TIN, M, NBI, G, E, D, AP, T, BT, PA, PB, QA, QB,
    loc, lev_sem, bot_s, bot_r, top_s, top_r, col_s, col_r, m_s, m_r, g_s, g_r, core_s, core_r,
):
    L, NBD, RC, CC = ITEMS
    BS = B * S
    NR = BS * NBD
    H = NBD // 2
    R8 = 2 * NBD
    blk, sub, lev = lax.axis_index("blk"), lax.axis_index("sub"), lax.axis_index("lev")
    me = blk * S + sub
    other = 1 - lev
    row = lax.broadcasted_iota(jnp.int32, (RC, CC), 0)
    lane = lax.broadcasted_iota(jnp.int32, (RC, CC), 1)

    def at_dev(d):
        return {"blk": d // S, "sub": d % S, "lev": lev}

    barrier = pltpu.get_barrier_semaphore()
    pl.semaphore_signal(barrier, inc=1, device_id={"lev": other}, device_id_type=pl.DeviceIdType.MESH)

    @pl.loop(1, BS)
    def _(d):
        pl.semaphore_signal(
            barrier, inc=1, device_id=at_dev((me + d) % BS), device_id_type=pl.DeviceIdType.MESH
        )

    load = pltpu.make_async_copy(tr, X.at[:, 1 : L + 1], loc.at[0])
    load.start()

    def remote(src, dst, ss, rs, dev):
        return pltpu.make_async_remote_copy(
            src_ref=src, dst_ref=dst, send_sem=ss, recv_sem=rs, device_id=dev,
            device_id_type=pl.DeviceIdType.MESH,
        )

    to_core = {"lev": other}
    MR = H * RC
    for j in range(H):
        M[me, lev, j * RC : (j + 1) * RC, :] = sd[lev * H + j]
    r8 = lax.broadcasted_iota(jnp.int32, (H * 4, CC), 0)
    lists = jnp.zeros((H * 4, CC), jnp.int32)
    for j in range(H):
        for s in range(4):
            lists = jnp.where(r8 == j * 4 + s, nb[lev * H + j, s], lists)
    M[me, lev, MR : MR + H * 4, :] = lists.astype(F32)

    zero_edge = jnp.zeros((S, R8, L * CC), F32)
    zero_block = jnp.zeros((RC, CC), F32)

    @pl.when(blk == 0)
    def _():
        BOTS[0:S] = zero_edge

    @pl.when(blk == B - 1)
    def _():
        TOPS[S : 2 * S] = zero_edge

    @pl.when(me == 0)
    def _():
        CR[0] = zero_block

    @pl.when(me == BS - 1)
    def _():
        CR[1] = zero_block

    outer = lev * (L + 1)
    for t in range(2):
        for b in range(NBD):
            X[t, outer, b] = zero_block

    load.wait()
    pl.semaphore_wait(barrier, BS)

    level_copy = remote(
        tr.at[:, pl.ds(other * (L - 1), 1)],
        X.at[:, pl.ds(lev * (L + 1), 1)],
        lev_sem.at[0], lev_sem.at[1], to_core,
    )
    level_copy.start()

    my_top = sub
    my_bot = S + sub

    def pack(k, packed):
        first, last = packed
        lanes = pl.ds(pl.multiple_of(k * CC, CC), CC)
        for t in range(2):
            for b in range(NBD):
                TOPS[my_top, t * NBD + b : t * NBD + b + 1, lanes] = X[t, k + 1, b, 0:1, :]
                BOTS[my_bot, t * NBD + b : t * NBD + b + 1, lanes] = X[t, k + 1, b, RC - 1 : RC, :]
            spot = t * L + k
            mine = lax.shift_right_logical(lane, 1) == spot
            first = jnp.where(mine, pltpu.roll(X[t, k + 1, 0], 2 * spot + 1, 1), first)
            last = jnp.where(mine, pltpu.roll(X[t, k + 1, NBD - 1], 2 * spot + 1, 1), last)
        return first, last

    first, last = lax.fori_loop(0, L, pack, (zero_block, zero_block))
    CP[0] = first
    CP[1] = last

    def top_slot(i):
        return TOPS.at[i]

    def bot_slot(i):
        return BOTS.at[i]

    def bot_to(i):
        return remote(
            bot_slot(S + sub), bot_slot(sub + (S if i < S else 0)), bot_s.at[i],
            bot_r.at[sub + (S if i < S else 0)],
            {"blk": blk + (0 if i < S else 1), "sub": i % S, "lev": lev},
        )

    def top_to(i):
        return remote(
            top_slot(sub), top_slot(sub + (0 if i < S else S)), top_s.at[i],
            top_r.at[sub + (0 if i < S else S)],
            {"blk": blk - (0 if i < S else 1), "sub": i % S, "lev": lev},
        )

    def each_edge(act):
        for i in range(S, 2 * S):
            pl.when(blk < B - 1)(lambda i=i: act(bot_to(i)))
            pl.when(blk > 0)(lambda i=i: act(top_to(i)))
        for i in range(S):
            pl.when(sub != i)(lambda i=i: act(bot_to(i)))
            pl.when(sub != i)(lambda i=i: act(top_to(i)))

    def col_down():
        return remote(CP.at[0], CR.at[1], col_s.at[0], col_r.at[1], at_dev(jnp.maximum(me - 1, 0)))

    def col_up():
        return remote(CP.at[1], CR.at[0], col_s.at[1], col_r.at[0], at_dev(jnp.minimum(me + 1, BS - 1)))

    each_edge(lambda c: c.start())
    pl.when(me > 0)(lambda: col_down().start())
    pl.when(me < BS - 1)(lambda: col_up().start())

    def m_to(d):
        dev = (me + d) % BS
        return remote(M.at[me, lev], M.at[me, lev], m_s.at[dev], m_r.at[me], at_dev(dev))

    def m_from(d):
        dev = (me + d) % BS
        return remote(M.at[dev, lev], M.at[dev, lev], m_s.at[dev], m_r.at[dev], at_dev(dev))

    @pl.loop(1, BS)
    def _(d):
        m_to(d).start()

    n8 = lax.broadcasted_iota(jnp.int32, (R8, 2 * S * R8), 0)
    c8 = lax.broadcasted_iota(jnp.int32, (R8, 2 * S * R8), 1)
    nba = jnp.zeros((R8, 2 * S * R8), jnp.int32)
    nbb = jnp.zeros((R8, 2 * S * R8), jnp.int32)
    for b in range(NBD):
        nba = jnp.where(n8 % NBD == b, nb[b, 0], nba)
        nbb = jnp.where(n8 % NBD == b, nb[b, 1], nbb)
    same_t = (n8 // NBD) == ((c8 // NBD) % 2)
    place = (c8 // R8) * NBD + c8 % NBD
    base = blk * S * NBD
    sel_a = jnp.where(same_t & (nba == place + base - S * NBD), 1.0, 0.0)
    sel_b = jnp.where(same_t & (nbb == place + base), 1.0, 0.0)

    for i in range(S):
        pl.when(blk > 0)(lambda i=i: remote(bot_slot(i), bot_slot(i), bot_s.at[i], bot_r.at[i], to_core).wait_recv())
        pl.when(sub != i)(
            lambda i=i: remote(bot_slot(S + i), bot_slot(S + i), bot_s.at[i], bot_r.at[S + i], to_core).wait_recv()
        )
        pl.when(sub != i)(lambda i=i: remote(top_slot(i), top_slot(i), top_s.at[i], top_r.at[i], to_core).wait_recv())
        pl.when(blk < B - 1)(
            lambda i=i: remote(top_slot(S + i), top_slot(S + i), top_s.at[i], top_r.at[S + i], to_core).wait_recv()
        )
    pl.when(me > 0)(lambda: remote(CR.at[0], CR.at[0], col_s.at[0], col_r.at[0], to_core).wait_recv())
    pl.when(me < BS - 1)(lambda: remote(CR.at[1], CR.at[1], col_s.at[1], col_r.at[1], to_core).wait_recv())
    level_copy.wait_recv()

    picked_a = jnp.dot(sel_a, BOTS[...].reshape(2 * S * R8, L * CC), precision=HIGH, preferred_element_type=F32)
    picked_b = jnp.dot(sel_b, TOPS[...].reshape(2 * S * R8, L * CC), precision=HIGH, preferred_element_type=F32)
    w8 = lax.broadcasted_iota(jnp.int32, (R8, L * CC), 0)
    open_a = jnp.zeros((R8, L * CC), jnp.int32)
    open_b = jnp.zeros((R8, L * CC), jnp.int32)
    for b in range(NBD):
        open_a = jnp.where(w8 % NBD == b, nb[b, 0], open_a)
        open_b = jnp.where(w8 % NBD == b, nb[b, 1], open_b)
    HA[...] = jnp.where(open_a < 0, TOPS[my_top], picked_a)
    HB[...] = jnp.where(open_b < 0, BOTS[my_bot], picked_b)

    wests = [jnp.full((RC, CC), nb[b, 2], jnp.int32) for b in range(NBD)]
    easts = [jnp.full((RC, CC), nb[b, 3], jnp.int32) for b in range(NBD)]
    levels = lt.shape[0]

    def step(k, cols):
        lanes = pl.ds(pl.multiple_of(k * CC, CC), CC)
        g = lev * L + k
        above = jnp.where(g == 0, 0.0, vm[jnp.maximum(g - 1, 0)])
        below = jnp.where(g == levels - 1, 0.0, vm[jnp.minimum(g, levels - 2)])
        thick = lt[g]
        new = []
        ends = []
        for t in range(2):
            shift = CC - 1 - 2 * (t * L + k)
            ends.append((pltpu.roll(CR[0], shift, 1), pltpu.roll(CR[1], shift, 1)))
        for b in range(NBD):
            q = me * NBD + b
            nxt = []
            for t in range(2):
                v = X[t, k + 1, b]
                before = ends[t][0] if b == 0 else X[t, k + 1, b - 1]
                after = ends[t][1] if b == NBD - 1 else X[t, k + 1, b + 1]
                spread = five_point(
                    v, before, after, HA[t * NBD + b : t * NBD + b + 1, lanes],
                    HB[t * NBD + b : t * NBD + b + 1, lanes], wests[b], easts[b], q, row, lane,
                )
                vertical = below * (X[t, k + 2, b] - v) - above * (v - X[t, k, b])
                y = v + hd[b] * spread + vertical
                Y[t, k, b] = y
                nxt.append(y)
            weighted = thick * (0.6 * nxt[0] + 0.05 * nxt[0] * nxt[0] - 0.8 * nxt[1])
            col = cols[b] + weighted
            C[k, b] = col
            new.append(col)
        return tuple(new)

    totals = lax.fori_loop(0, L, step, (zero_block,) * NBD)
    for b in range(NBD):
        TOT[b] = totals[b]
    tot_copy = remote(TOT, TIN, core_s.at[0], core_r.at[0], to_core)
    tot_copy.start()
    store = pltpu.make_async_copy(Y, out_tr, loc.at[1])
    store.start()

    @pl.loop(1, BS)
    def _(d):
        m_from(d).wait_recv()

    m_core = remote(M.at[:, lev], M.at[:, lev], core_s.at[1], core_r.at[1], to_core)
    m_core.start()

    tot_copy.wait_recv()
    for j in range(H):
        G[me, lev, j] = TOT[lev * H + j] + TIN[lev * H + j]

    def g_to(d):
        dev = (me + d) % BS
        return remote(G.at[me, lev], G.at[me, lev], g_s.at[dev], g_r.at[me], at_dev(dev))

    def g_from(d):
        dev = (me + d) % BS
        return remote(G.at[dev, lev], G.at[dev, lev], g_s.at[dev], g_r.at[dev], at_dev(dev))

    @pl.loop(1, BS)
    def _(d):
        g_to(d).start()

    remote(M.at[:, other], M.at[:, other], core_s.at[1], core_r.at[1], to_core).wait_recv()

    @pl.loop(0, BS)
    def _(d):
        for l in range(2):
            NBI[pl.ds(pl.multiple_of(d * NBD * 4 + l * H * 4, 8), H * 4), :] = M[
                d, l, MR : MR + H * 4, :
            ].astype(jnp.int32)

    KP = T.shape[0]
    PA[...] = NBI[pl.ds(0, NR, stride=4), :]
    PB[...] = NBI[pl.ds(1, NR, stride=4), :]
    wide = lax.broadcasted_iota(jnp.int32, (NR, CC), 1)
    for c in range(KP // CC):
        QA[:, c * CC : (c + 1) * CC] = jnp.where(PA[...] == wide + c * CC, 1.0, 0.0)
        QB[:, c * CC : (c + 1) * CC] = jnp.where(PB[...] == wide + c * CC, 1.0, 0.0)
    if KP > NR:
        T[NR:KP, :] = jnp.zeros((KP - NR, CC), F32)
        BT[NR:KP, :] = jnp.zeros((KP - NR, CC), F32)
    D[0] = zero_block
    D[NR + 1] = zero_block

    @pl.loop(1, BS)
    def _(d):
        g_from(d).wait_recv()

    g_core = remote(G.at[:, lev], G.at[:, lev], core_s.at[2], core_r.at[2], to_core)
    g_core.start()
    remote(G.at[:, other], G.at[:, other], core_s.at[2], core_r.at[2], to_core).wait_recv()
    g_core.wait_send()

    @pl.loop(1, BS)
    def _(d):
        g_to(d).wait_send()

    def total(acc):
        return jnp.sum(jnp.sum(acc, axis=0, keepdims=True), axis=1, keepdims=True)

    def over_blocks(body, carry):
        def devs(d, carry):
            for b in range(NBD):
                carry = body(d, b, d * NBD + b, carry)
            return carry

        return lax.fori_loop(0, BS, devs, carry)

    def set_direction(q, d):
        D[q + 1] = d
        T[pl.ds(q, 1), :] = d[0:1, :]
        BT[pl.ds(q, 1), :] = d[RC - 1 : RC, :]

    def begin(d, b, q, acc):
        f = G[d, b // H, b % H]
        set_direction(q, f)
        E[q] = zero_block
        return acc + f * f

    norm_now = total(over_blocks(begin, zero_block))
    for iteration in range(ITERS):
        tops, bots = T[...], BT[...]
        up_rows = jnp.dot(QA[...], bots, precision=HIGH, preferred_element_type=F32)
        down_rows = jnp.dot(QB[...], tops, precision=HIGH, preferred_element_type=F32)
        HA2 = jnp.where(PA[...] < 0, T[0:NR, :], up_rows)
        HB2 = jnp.where(PB[...] < 0, BT[0:NR, :], down_rows)
        AP[NR] = zero_block
        T[0:NR, :] = HA2
        BT[0:NR, :] = HB2

        def apply(d, b, q, acc):
            v = D[q + 1]
            west = jnp.broadcast_to(NBI[pl.ds(q * 4 + 2, 1), :], (RC, CC))
            east = jnp.broadcast_to(NBI[pl.ds(q * 4 + 3, 1), :], (RC, CC))
            spread = five_point(
                v, D[q], D[q + 2], T[pl.ds(q, 1), :], BT[pl.ds(q, 1), :], west, east, q, row, lane
            )
            diag = M[d, b // H, (b % H) * RC : (b % H + 1) * RC, :]
            applied = diag * v - spread
            AP[q] = applied
            return acc + v * applied

        size = norm_now / total(over_blocks(apply, zero_block))

        def update(d, b, q, acc):
            E[q] = E[q] + size * D[q + 1]
            r = G[d, b // H, b % H] - size * AP[q]
            G[d, b // H, b % H] = r
            return acc + r * r

        if iteration == ITERS - 1:
            def finish(d, b, q, acc):
                E[q] = E[q] + size * D[q + 1]
                return acc

            over_blocks(finish, jnp.int32(0))
            break
        norm_next = total(over_blocks(update, zero_block))
        beta = norm_next / norm_now

        def turn(d, b, q, acc):
            set_direction(q, G[d, b // H, b % H] + beta * D[q + 1])
            return acc

        over_blocks(turn, jnp.int32(0))
        norm_now = norm_next

    levf = lev.astype(F32)
    eta = [E[me * NBD + b] - levf * TIN[b] for b in range(NBD)]

    def press(k, _):
        for b in range(NBD):
            C[k, b] = eta[b] - C[k, b]
        return 0

    lax.fori_loop(0, L, press, 0)
    p_store = pltpu.make_async_copy(C, out_p, loc.at[2])
    p_store.start()
    for s in range(baro.shape[0]):
        held = baro[s]
        out_s[s] = jnp.where(jnp.full((RC, CC), held, jnp.int32) >= 0, E[jnp.maximum(held, 0)], 0.0)

    level_copy.wait_send()
    each_edge(lambda c: c.wait_send())
    pl.when(me > 0)(lambda: col_down().wait_send())
    pl.when(me < BS - 1)(lambda: col_up().wait_send())

    @pl.loop(1, BS)
    def _(d):
        m_to(d).wait_send()

    tot_copy.wait_send()
    m_core.wait_send()
    store.wait()
    p_store.wait()


def local(tracers, horizontal_diffusivity, vertical_mixing, layer_thickness, surface_diagonal, neighbours, baro_blocks):
    B, S = lax.axis_size("blk"), lax.axis_size("sub")
    L, NBD, RC, CC = tracers.shape[1:]
    BS = B * S
    NR = BS * NBD
    H = NBD // 2
    R8 = 2 * NBD
    KP = -(-NR // CC) * CC
    vm = pltpu.VMEM
    dma = pltpu.SemaphoreType.DMA
    slots = baro_blocks.shape[0]
    scratch = [
        vm((2, L + 2, NBD, RC, CC), F32),
        vm((2, L, NBD, RC, CC), F32),
        vm((L, NBD, RC, CC), F32),
        vm((2 * S, R8, L * CC), F32),
        vm((2 * S, R8, L * CC), F32),
        vm((R8, L * CC), F32),
        vm((R8, L * CC), F32),
        vm((2, RC, CC), F32),
        vm((2, RC, CC), F32),
        vm((NBD, RC, CC), F32),
        vm((NBD, RC, CC), F32),
        vm((BS, 2, H * RC + H * 4, CC), F32),
        vm((NR * 4, CC), jnp.int32),
        vm((BS, 2, H, RC, CC), F32),
        vm((NR, RC, CC), F32),
        vm((NR + 2, RC, CC), F32),
        vm((NR + 1, RC, CC), F32),
        vm((KP, CC), F32),
        vm((KP, CC), F32),
        vm((NR, CC), jnp.int32),
        vm((NR, CC), jnp.int32),
        vm((NR, KP), F32),
        vm((NR, KP), F32),
        dma((3,)), dma((2,)), dma((2 * S,)), dma((2 * S,)), dma((2 * S,)), dma((2 * S,)),
        dma((2,)), dma((2,)), dma((BS,)), dma((BS,)), dma((BS,)), dma((BS,)), dma((3,)), dma((3,)),
    ]
    need = (10 * L * NBD + 7 * NR) * RC * CC * 4 + 4 * NR * KP * 4 + (8 << 20)
    smem = pl.BlockSpec(memory_space=pltpu.SMEM)
    vmem = pl.BlockSpec(memory_space=pltpu.VMEM)
    hbm = pl.BlockSpec(memory_space=pl.ANY)
    return pl.pallas_call(
        functools.partial(kernel, B, S, (L, NBD, RC, CC)),
        out_shape=(
            jax.ShapeDtypeStruct(tracers.shape, F32),
            jax.ShapeDtypeStruct((L, NBD, RC, CC), F32),
            jax.ShapeDtypeStruct((slots, RC, CC), F32),
        ),
        in_specs=[hbm, vmem, smem, smem, vmem, smem, smem],
        out_specs=(hbm, hbm, vmem),
        scratch_shapes=scratch,
        compiler_params=pltpu.CompilerParams(
            collective_id=0, has_side_effects=True, vmem_limit_bytes=need
        ),
    )(tracers, horizontal_diffusivity, vertical_mixing, layer_thickness, surface_diagonal, neighbours, baro_blocks)


def solution(mesh):
    placed = (
        P("grp", "lev", ("blk", "sub"), None, None),
        P(("blk", "sub"), None, None),
        P(),
        P(),
        P(("blk", "sub"), None, None),
        P(("blk", "sub"), None),
        P(("blk", "sub", "lev")),
    )
    return jax.shard_map(
        local,
        mesh=mesh,
        in_specs=placed,
        out_specs=(
            P("grp", "lev", ("blk", "sub"), None, None),
            P(("grp", "lev"), ("blk", "sub"), None, None),
            P(("grp", "blk", "sub", "lev"), None, None),
        ),
        check_vma=False,
    )
```

```python
import functools

import jax
import jax.numpy as jnp
from jax import lax
from jax.experimental import pallas as pl
from jax.experimental.pallas import tpu as pltpu
from jax.sharding import PartitionSpec as P

ITERS = 3
F32 = jnp.float32
HIGH = lax.Precision.HIGHEST


def five_point(v, before, after, up, down, west, east, q, row, lane):
    rows, cols = v.shape
    xw = jnp.where(lane == cols - 1, jnp.where(west == q - 1, before, after), v)
    xe = jnp.where(lane == 0, jnp.where(east == q - 1, before, after), v)
    dw = jnp.where((lane == 0) & (west < 0), 0.0, pltpu.roll(xw, 1, 1) - v)
    de = jnp.where((lane == cols - 1) & (east < 0), 0.0, pltpu.roll(xe, cols - 1, 1) - v)
    fa = jnp.where(row == 0, jnp.broadcast_to(up, v.shape), pltpu.roll(v, 1, 0))
    fb = jnp.where(row == rows - 1, jnp.broadcast_to(down, v.shape), pltpu.roll(v, rows - 1, 0))
    return (fa - v) + (fb - v) + dw + de


def kernel(
    B, S, ITEMS,
    tr, hd_in, vm_in, lt_in, sd_in, nb_in, baro_in,
    Y, C, out_s,
    hd, vm, lt, sd, nb, baro, X, TOPS, BOTS, HA, HB, CP, CR, TOT, TIN, M, NBI, G, E, D, AP, T, BT, PA, PB, QA, QB,
    loc, lev_sem, bot_s, bot_r, top_s, top_r, col_s, col_r, m_s, m_r, g_s, g_r, core_s, core_r,
):
    L, NBD, RC, CC = ITEMS
    BS = B * S
    NR = BS * NBD
    H = NBD // 2
    R8 = 2 * NBD
    blk, sub, lev = lax.axis_index("blk"), lax.axis_index("sub"), lax.axis_index("lev")
    me = blk * S + sub
    other = 1 - lev
    row = lax.broadcasted_iota(jnp.int32, (RC, CC), 0)
    lane = lax.broadcasted_iota(jnp.int32, (RC, CC), 1)

    def at_dev(d):
        return {"blk": d // S, "sub": d % S, "lev": lev}

    load = pltpu.make_async_copy(tr, X.at[:, 1 : L + 1], loc.at[0])
    load.start()
    small = [
        pltpu.make_async_copy(source, target, loc.at[1 + i])
        for i, (source, target) in enumerate(
            [(nb_in, nb), (sd_in, sd), (hd_in, hd), (vm_in, vm), (lt_in, lt), (baro_in, baro)]
        )
    ]
    for copy in small:
        copy.start()

    barrier = pltpu.get_barrier_semaphore()
    pl.semaphore_signal(barrier, inc=1, device_id={"lev": other}, device_id_type=pl.DeviceIdType.MESH)

    @pl.loop(1, BS)
    def _(d):
        pl.semaphore_signal(
            barrier, inc=1, device_id=at_dev((me + d) % BS), device_id_type=pl.DeviceIdType.MESH
        )


    def remote(src, dst, ss, rs, dev):
        return pltpu.make_async_remote_copy(
            src_ref=src, dst_ref=dst, send_sem=ss, recv_sem=rs, device_id=dev,
            device_id_type=pl.DeviceIdType.MESH,
        )

    to_core = {"lev": other}
    for copy in small:
        copy.wait()
    MR = H * RC
    for j in range(H):
        M[me, lev, j * RC : (j + 1) * RC, :] = sd[lev * H + j]
    r8 = lax.broadcasted_iota(jnp.int32, (H * 4, CC), 0)
    lists = jnp.zeros((H * 4, CC), jnp.int32)
    for j in range(H):
        for s in range(4):
            lists = jnp.where(r8 == j * 4 + s, nb[lev * H + j, s], lists)
    M[me, lev, MR : MR + H * 4, :] = lists.astype(F32)

    zero_edge = jnp.zeros((S, R8, L * CC), F32)
    zero_block = jnp.zeros((RC, CC), F32)

    @pl.when(blk == 0)
    def _():
        BOTS[0:S] = zero_edge

    @pl.when(blk == B - 1)
    def _():
        TOPS[S : 2 * S] = zero_edge

    @pl.when(me == 0)
    def _():
        CR[0] = zero_block

    @pl.when(me == BS - 1)
    def _():
        CR[1] = zero_block

    outer = lev * (L + 1)
    for t in range(2):
        for b in range(NBD):
            X[t, outer, b] = zero_block

    load.wait()
    pl.semaphore_wait(barrier, BS)

    level_copy = remote(
        tr.at[:, pl.ds(other * (L - 1), 1)],
        X.at[:, pl.ds(lev * (L + 1), 1)],
        lev_sem.at[0], lev_sem.at[1], to_core,
    )
    level_copy.start()

    my_top = sub
    my_bot = S + sub

    def pack(k, packed):
        first, last = packed
        lanes = pl.ds(pl.multiple_of(k * CC, CC), CC)
        for t in range(2):
            for b in range(NBD):
                TOPS[my_top, t * NBD + b : t * NBD + b + 1, lanes] = X[t, k + 1, b, 0:1, :]
                BOTS[my_bot, t * NBD + b : t * NBD + b + 1, lanes] = X[t, k + 1, b, RC - 1 : RC, :]
            spot = t * L + k
            mine = lax.shift_right_logical(lane, 1) == spot
            first = jnp.where(mine, pltpu.roll(X[t, k + 1, 0], 2 * spot + 1, 1), first)
            last = jnp.where(mine, pltpu.roll(X[t, k + 1, NBD - 1], 2 * spot + 1, 1), last)
        return first, last

    first, last = lax.fori_loop(0, L, pack, (zero_block, zero_block))
    CP[0] = first
    CP[1] = last

    def top_slot(i):
        return TOPS.at[i]

    def bot_slot(i):
        return BOTS.at[i]

    def bot_to(i):
        return remote(
            bot_slot(S + sub), bot_slot(sub + (S if i < S else 0)), bot_s.at[i],
            bot_r.at[sub + (S if i < S else 0)],
            {"blk": blk + (0 if i < S else 1), "sub": i % S, "lev": lev},
        )

    def top_to(i):
        return remote(
            top_slot(sub), top_slot(sub + (0 if i < S else S)), top_s.at[i],
            top_r.at[sub + (0 if i < S else S)],
            {"blk": blk - (0 if i < S else 1), "sub": i % S, "lev": lev},
        )

    def each_edge(act):
        for i in range(S, 2 * S):
            pl.when(blk < B - 1)(lambda i=i: act(bot_to(i)))
            pl.when(blk > 0)(lambda i=i: act(top_to(i)))
        for i in range(S):
            pl.when(sub != i)(lambda i=i: act(bot_to(i)))
            pl.when(sub != i)(lambda i=i: act(top_to(i)))

    def col_down():
        return remote(CP.at[0], CR.at[1], col_s.at[0], col_r.at[1], at_dev(jnp.maximum(me - 1, 0)))

    def col_up():
        return remote(CP.at[1], CR.at[0], col_s.at[1], col_r.at[0], at_dev(jnp.minimum(me + 1, BS - 1)))

    each_edge(lambda c: c.start())
    pl.when(me > 0)(lambda: col_down().start())
    pl.when(me < BS - 1)(lambda: col_up().start())

    def m_to(d):
        dev = (me + d) % BS
        return remote(M.at[me, lev], M.at[me, lev], m_s.at[dev], m_r.at[me], at_dev(dev))

    def m_from(d):
        dev = (me + d) % BS
        return remote(M.at[dev, lev], M.at[dev, lev], m_s.at[dev], m_r.at[dev], at_dev(dev))

    @pl.loop(1, BS)
    def _(d):
        m_to(d).start()

    n8 = lax.broadcasted_iota(jnp.int32, (R8, 2 * S * R8), 0)
    c8 = lax.broadcasted_iota(jnp.int32, (R8, 2 * S * R8), 1)
    nba = jnp.zeros((R8, 2 * S * R8), jnp.int32)
    nbb = jnp.zeros((R8, 2 * S * R8), jnp.int32)
    for b in range(NBD):
        nba = jnp.where(n8 % NBD == b, nb[b, 0], nba)
        nbb = jnp.where(n8 % NBD == b, nb[b, 1], nbb)
    same_t = (n8 // NBD) == ((c8 // NBD) % 2)
    place = (c8 // R8) * NBD + c8 % NBD
    base = blk * S * NBD
    sel_a = jnp.where(same_t & (nba == place + base - S * NBD), 1.0, 0.0)
    sel_b = jnp.where(same_t & (nbb == place + base), 1.0, 0.0)

    for i in range(S):
        pl.when(blk > 0)(lambda i=i: remote(bot_slot(i), bot_slot(i), bot_s.at[i], bot_r.at[i], to_core).wait_recv())
        pl.when(sub != i)(
            lambda i=i: remote(bot_slot(S + i), bot_slot(S + i), bot_s.at[i], bot_r.at[S + i], to_core).wait_recv()
        )
        pl.when(sub != i)(lambda i=i: remote(top_slot(i), top_slot(i), top_s.at[i], top_r.at[i], to_core).wait_recv())
        pl.when(blk < B - 1)(
            lambda i=i: remote(top_slot(S + i), top_slot(S + i), top_s.at[i], top_r.at[S + i], to_core).wait_recv()
        )
    pl.when(me > 0)(lambda: remote(CR.at[0], CR.at[0], col_s.at[0], col_r.at[0], to_core).wait_recv())
    pl.when(me < BS - 1)(lambda: remote(CR.at[1], CR.at[1], col_s.at[1], col_r.at[1], to_core).wait_recv())
    level_copy.wait_recv()

    picked_a = jnp.dot(sel_a, BOTS[...].reshape(2 * S * R8, L * CC), precision=HIGH, preferred_element_type=F32)
    picked_b = jnp.dot(sel_b, TOPS[...].reshape(2 * S * R8, L * CC), precision=HIGH, preferred_element_type=F32)
    w8 = lax.broadcasted_iota(jnp.int32, (R8, L * CC), 0)
    open_a = jnp.zeros((R8, L * CC), jnp.int32)
    open_b = jnp.zeros((R8, L * CC), jnp.int32)
    for b in range(NBD):
        open_a = jnp.where(w8 % NBD == b, nb[b, 0], open_a)
        open_b = jnp.where(w8 % NBD == b, nb[b, 1], open_b)
    HA[...] = jnp.where(open_a < 0, TOPS[my_top], picked_a)
    HB[...] = jnp.where(open_b < 0, BOTS[my_bot], picked_b)

    wests = [jnp.full((RC, CC), nb[b, 2], jnp.int32) for b in range(NBD)]
    easts = [jnp.full((RC, CC), nb[b, 3], jnp.int32) for b in range(NBD)]
    levels = lt.shape[0]

    def step(k, cols):
        lanes = pl.ds(pl.multiple_of(k * CC, CC), CC)
        g = lev * L + k
        above = jnp.where(g == 0, 0.0, vm[jnp.maximum(g - 1, 0)])
        below = jnp.where(g == levels - 1, 0.0, vm[jnp.minimum(g, levels - 2)])
        thick = lt[g]
        new = []
        ends = []
        for t in range(2):
            shift = CC - 1 - 2 * (t * L + k)
            ends.append((pltpu.roll(CR[0], shift, 1), pltpu.roll(CR[1], shift, 1)))
        for b in range(NBD):
            q = me * NBD + b
            nxt = []
            for t in range(2):
                v = X[t, k + 1, b]
                before = ends[t][0] if b == 0 else X[t, k + 1, b - 1]
                after = ends[t][1] if b == NBD - 1 else X[t, k + 1, b + 1]
                spread = five_point(
                    v, before, after, HA[t * NBD + b : t * NBD + b + 1, lanes],
                    HB[t * NBD + b : t * NBD + b + 1, lanes], wests[b], easts[b], q, row, lane,
                )
                vertical = below * (X[t, k + 2, b] - v) - above * (v - X[t, k, b])
                y = v + hd[b] * spread + vertical
                Y[t, k, b] = y
                nxt.append(y)
            weighted = thick * (0.6 * nxt[0] + 0.05 * nxt[0] * nxt[0] - 0.8 * nxt[1])
            col = cols[b] + weighted
            C[k, b] = col
            new.append(col)
        return tuple(new)

    totals = lax.fori_loop(0, L, step, (zero_block,) * NBD)
    for b in range(NBD):
        TOT[b] = totals[b]
    tot_copy = remote(TOT, TIN, core_s.at[0], core_r.at[0], to_core)
    tot_copy.start()

    @pl.loop(1, BS)
    def _(d):
        m_from(d).wait_recv()

    m_core = remote(M.at[:, lev], M.at[:, lev], core_s.at[1], core_r.at[1], to_core)
    m_core.start()

    tot_copy.wait_recv()
    for j in range(H):
        G[me, lev, j] = TOT[lev * H + j] + TIN[lev * H + j]

    def g_to(d):
        dev = (me + d) % BS
        return remote(G.at[me, lev], G.at[me, lev], g_s.at[dev], g_r.at[me], at_dev(dev))

    def g_from(d):
        dev = (me + d) % BS
        return remote(G.at[dev, lev], G.at[dev, lev], g_s.at[dev], g_r.at[dev], at_dev(dev))

    @pl.loop(1, BS)
    def _(d):
        g_to(d).start()

    remote(M.at[:, other], M.at[:, other], core_s.at[1], core_r.at[1], to_core).wait_recv()

    @pl.loop(0, BS)
    def _(d):
        for l in range(2):
            NBI[pl.ds(pl.multiple_of(d * NBD * 4 + l * H * 4, 8), H * 4), :] = M[
                d, l, MR : MR + H * 4, :
            ].astype(jnp.int32)

    KP = T.shape[0]
    PA[...] = NBI[pl.ds(0, NR, stride=4), :]
    PB[...] = NBI[pl.ds(1, NR, stride=4), :]
    wide = lax.broadcasted_iota(jnp.int32, (NR, CC), 1)
    for c in range(KP // CC):
        QA[:, c * CC : (c + 1) * CC] = jnp.where(PA[...] == wide + c * CC, 1.0, 0.0)
        QB[:, c * CC : (c + 1) * CC] = jnp.where(PB[...] == wide + c * CC, 1.0, 0.0)
    if KP > NR:
        T[NR:KP, :] = jnp.zeros((KP - NR, CC), F32)
        BT[NR:KP, :] = jnp.zeros((KP - NR, CC), F32)
    D[0] = zero_block
    D[NR + 1] = zero_block

    @pl.loop(1, BS)
    def _(d):
        g_from(d).wait_recv()

    g_core = remote(G.at[:, lev], G.at[:, lev], core_s.at[2], core_r.at[2], to_core)
    g_core.start()
    remote(G.at[:, other], G.at[:, other], core_s.at[2], core_r.at[2], to_core).wait_recv()
    g_core.wait_send()

    @pl.loop(1, BS)
    def _(d):
        g_to(d).wait_send()

    def total(acc):
        return jnp.sum(jnp.sum(acc, axis=0, keepdims=True), axis=1, keepdims=True)

    def over_blocks(body, carry):
        def devs(d, carry):
            for b in range(NBD):
                carry = body(d, b, d * NBD + b, carry)
            return carry

        return lax.fori_loop(0, BS, devs, carry)

    def set_direction(q, d):
        D[q + 1] = d
        T[pl.ds(q, 1), :] = d[0:1, :]
        BT[pl.ds(q, 1), :] = d[RC - 1 : RC, :]

    def begin(d, b, q, acc):
        f = G[d, b // H, b % H]
        set_direction(q, f)
        E[q] = zero_block
        return acc + f * f

    norm_now = total(over_blocks(begin, zero_block))
    for iteration in range(ITERS):
        tops, bots = T[...], BT[...]
        up_rows = jnp.dot(QA[...], bots, precision=HIGH, preferred_element_type=F32)
        down_rows = jnp.dot(QB[...], tops, precision=HIGH, preferred_element_type=F32)
        HA2 = jnp.where(PA[...] < 0, T[0:NR, :], up_rows)
        HB2 = jnp.where(PB[...] < 0, BT[0:NR, :], down_rows)
        AP[NR] = zero_block
        T[0:NR, :] = HA2
        BT[0:NR, :] = HB2

        def apply(d, b, q, acc):
            v = D[q + 1]
            west = jnp.broadcast_to(NBI[pl.ds(q * 4 + 2, 1), :], (RC, CC))
            east = jnp.broadcast_to(NBI[pl.ds(q * 4 + 3, 1), :], (RC, CC))
            spread = five_point(
                v, D[q], D[q + 2], T[pl.ds(q, 1), :], BT[pl.ds(q, 1), :], west, east, q, row, lane
            )
            diag = M[d, b // H, (b % H) * RC : (b % H + 1) * RC, :]
            applied = diag * v - spread
            AP[q] = applied
            return acc + v * applied

        size = norm_now / total(over_blocks(apply, zero_block))

        def update(d, b, q, acc):
            E[q] = E[q] + size * D[q + 1]
            r = G[d, b // H, b % H] - size * AP[q]
            G[d, b // H, b % H] = r
            return acc + r * r

        if iteration == ITERS - 1:
            def finish(d, b, q, acc):
                E[q] = E[q] + size * D[q + 1]
                return acc

            over_blocks(finish, jnp.int32(0))
            break
        norm_next = total(over_blocks(update, zero_block))
        beta = norm_next / norm_now

        def turn(d, b, q, acc):
            set_direction(q, G[d, b // H, b % H] + beta * D[q + 1])
            return acc

        over_blocks(turn, jnp.int32(0))
        norm_now = norm_next

    levf = lev.astype(F32)
    eta = [E[me * NBD + b] - levf * TIN[b] for b in range(NBD)]

    def press(k, _):
        for b in range(NBD):
            C[k, b] = eta[b] - C[k, b]
        return 0

    lax.fori_loop(0, L, press, 0)
    for s in range(baro.shape[0]):
        held = baro[s]
        out_s[s] = jnp.where(jnp.full((RC, CC), held, jnp.int32) >= 0, E[jnp.maximum(held, 0)], 0.0)

    level_copy.wait_send()
    each_edge(lambda c: c.wait_send())
    pl.when(me > 0)(lambda: col_down().wait_send())
    pl.when(me < BS - 1)(lambda: col_up().wait_send())

    @pl.loop(1, BS)
    def _(d):
        m_to(d).wait_send()

    tot_copy.wait_send()
    m_core.wait_send()


def local(tracers, horizontal_diffusivity, vertical_mixing, layer_thickness, surface_diagonal, neighbours, baro_blocks):
    B, S = lax.axis_size("blk"), lax.axis_size("sub")
    L, NBD, RC, CC = tracers.shape[1:]
    BS = B * S
    NR = BS * NBD
    H = NBD // 2
    R8 = 2 * NBD
    KP = -(-NR // CC) * CC
    vm = pltpu.VMEM
    dma = pltpu.SemaphoreType.DMA
    slots = baro_blocks.shape[0]
    smem = pltpu.SMEM
    scratch = [
        vm((NBD, RC, CC), F32),
        smem(vertical_mixing.shape, F32),
        smem(layer_thickness.shape, F32),
        vm((NBD, RC, CC), F32),
        smem(neighbours.shape, jnp.int32),
        smem(baro_blocks.shape, jnp.int32),
        vm((2, L + 2, NBD, RC, CC), F32),
        vm((2 * S, R8, L * CC), F32),
        vm((2 * S, R8, L * CC), F32),
        vm((R8, L * CC), F32),
        vm((R8, L * CC), F32),
        vm((2, RC, CC), F32),
        vm((2, RC, CC), F32),
        vm((NBD, RC, CC), F32),
        vm((NBD, RC, CC), F32),
        vm((BS, 2, H * RC + H * 4, CC), F32),
        vm((NR * 4, CC), jnp.int32),
        vm((BS, 2, H, RC, CC), F32),
        vm((NR, RC, CC), F32),
        vm((NR + 2, RC, CC), F32),
        vm((NR + 1, RC, CC), F32),
        vm((KP, CC), F32),
        vm((KP, CC), F32),
        vm((NR, CC), jnp.int32),
        vm((NR, CC), jnp.int32),
        vm((NR, KP), F32),
        vm((NR, KP), F32),
        dma((7,)), dma((2,)), dma((2 * S,)), dma((2 * S,)), dma((2 * S,)), dma((2 * S,)),
        dma((2,)), dma((2,)), dma((BS,)), dma((BS,)), dma((BS,)), dma((BS,)), dma((3,)), dma((3,)),
    ]
    need = (10 * L * NBD + 7 * NR) * RC * CC * 4 + 4 * NR * KP * 4 + (8 << 20)
    vmem = pl.BlockSpec(memory_space=pltpu.VMEM)
    hbm = pl.BlockSpec(memory_space=pltpu.HBM)
    shapes = (
        jax.ShapeDtypeStruct(tracers.shape, F32),
        jax.ShapeDtypeStruct((L, NBD, RC, CC), F32),
        jax.ShapeDtypeStruct((slots, RC, CC), F32),
    )
    results = pl.pallas_call(
        functools.partial(kernel, B, S, (L, NBD, RC, CC)),
        out_shape=shapes,
        in_specs=[hbm] * 7,
        out_specs=(vmem,) * 3,
        scratch_shapes=scratch,
        compiler_params=pltpu.CompilerParams(
            collective_id=0, has_side_effects=True, vmem_limit_bytes=need
        ),
    )(*[
        pltpu.with_memory_space_constraint(x, pltpu.HBM)
        for x in (
            tracers, horizontal_diffusivity, vertical_mixing, layer_thickness, surface_diagonal,
            neighbours, baro_blocks,
        )
    ])
    return pl.pallas_call(
        write_out,
        out_shape=shapes,
        in_specs=[vmem] * 3,
        out_specs=(hbm,) * 3,
        scratch_shapes=[dma((4,))],
        compiler_params=pltpu.CompilerParams(vmem_limit_bytes=8 << 20),
    )(*results)


def write_out(tr, p, s, out_tr, out_p, out_s, sem):
    copies = [
        pltpu.make_async_copy(tr.at[0], out_tr.at[0], sem.at[0]),
        pltpu.make_async_copy(tr.at[1], out_tr.at[1], sem.at[1]),
        pltpu.make_async_copy(p, out_p, sem.at[2]),
        pltpu.make_async_copy(s, out_s, sem.at[3]),
    ]
    for copy in copies:
        copy.start()
    for copy in copies:
        copy.wait()


def solution(mesh):
    placed = (
        P("grp", "lev", ("blk", "sub"), None, None),
        P(("blk", "sub"), None, None),
        P(),
        P(),
        P(("blk", "sub"), None, None),
        P(("blk", "sub"), None),
        P(("blk", "sub", "lev")),
    )
    return jax.shard_map(
        local,
        mesh=mesh,
        in_specs=placed,
        out_specs=(
            P("grp", "lev", ("blk", "sub"), None, None),
            P(("grp", "lev"), ("blk", "sub"), None, None),
            P(("grp", "blk", "sub", "lev"), None, None),
        ),
        check_vma=False,
    )
```

```python
import functools

import jax
import jax.numpy as jnp
from jax import lax
from jax.experimental import pallas as pl
from jax.experimental.pallas import tpu as pltpu
from jax.sharding import PartitionSpec as P

ITERS = 3
F32 = jnp.float32
HIGH = lax.Precision.HIGHEST


def five_point(v, before, after, up, down, west, east, q, row, lane):
    rows, cols = v.shape
    xw = jnp.where(lane == cols - 1, jnp.where(west == q - 1, before, after), v)
    xe = jnp.where(lane == 0, jnp.where(east == q - 1, before, after), v)
    dw = jnp.where((lane == 0) & (west < 0), 0.0, pltpu.roll(xw, 1, 1) - v)
    de = jnp.where((lane == cols - 1) & (east < 0), 0.0, pltpu.roll(xe, cols - 1, 1) - v)
    fa = jnp.where(row == 0, jnp.broadcast_to(up, v.shape), pltpu.roll(v, 1, 0))
    fb = jnp.where(row == rows - 1, jnp.broadcast_to(down, v.shape), pltpu.roll(v, rows - 1, 0))
    return (fa - v) + (fb - v) + dw + de


def kernel(
    B, S, ITEMS,
    tr, hd_in, vm_in, lt_in, sd_in, nb_in, baro_in,
    Y, C, out_s,
    hd, vm, lt, sd, nb, baro, X, TOPS, BOTS, HA, HB, CP, CR, TOT, TIN, M, NBI, G, D, AP, T, BT, PA, PB, QA, QB,
    loc, lev_sem, bot_s, bot_r, top_s, top_r, col_s, col_r, m_s, m_r, g_s, g_r, gc_s, gc_r, core_s, core_r,
):
    L, NBD, RC, CC = ITEMS
    BS = B * S
    NR = BS * NBD
    H = NBD // 2
    R8 = 2 * NBD
    blk, sub, lev = lax.axis_index("blk"), lax.axis_index("sub"), lax.axis_index("lev")
    me = blk * S + sub
    other = 1 - lev
    row = lax.broadcasted_iota(jnp.int32, (RC, CC), 0)
    lane = lax.broadcasted_iota(jnp.int32, (RC, CC), 1)

    def at_dev(d):
        return {"blk": d // S, "sub": d % S, "lev": lev}

    load = pltpu.make_async_copy(tr, X.at[:, 1 : L + 1], loc.at[0])
    load.start()
    small = [
        pltpu.make_async_copy(source, target, loc.at[1 + i])
        for i, (source, target) in enumerate(
            [(nb_in, nb), (sd_in, sd), (hd_in, hd), (vm_in, vm), (lt_in, lt), (baro_in, baro)]
        )
    ]
    for copy in small:
        copy.start()

    barrier = pltpu.get_barrier_semaphore()
    pl.semaphore_signal(barrier, inc=1, device_id={"lev": other}, device_id_type=pl.DeviceIdType.MESH)

    @pl.loop(1, BS)
    def _(d):
        pl.semaphore_signal(
            barrier, inc=1, device_id=at_dev((me + d) % BS), device_id_type=pl.DeviceIdType.MESH
        )


    def remote(src, dst, ss, rs, dev):
        return pltpu.make_async_remote_copy(
            src_ref=src, dst_ref=dst, send_sem=ss, recv_sem=rs, device_id=dev,
            device_id_type=pl.DeviceIdType.MESH,
        )

    to_core = {"lev": other}
    for copy in small:
        copy.wait()
    MR = H * RC
    for j in range(H):
        M[me, lev, j * RC : (j + 1) * RC, :] = sd[lev * H + j]
    r8 = lax.broadcasted_iota(jnp.int32, (H * 4, CC), 0)
    lists = jnp.zeros((H * 4, CC), jnp.int32)
    for j in range(H):
        for s in range(4):
            lists = jnp.where(r8 == j * 4 + s, nb[lev * H + j, s], lists)
    M[me, lev, MR : MR + H * 4, :] = lists.astype(F32)

    zero_edge = jnp.zeros((S, R8, L * CC), F32)
    zero_block = jnp.zeros((RC, CC), F32)

    @pl.when(blk == 0)
    def _():
        BOTS[0:S] = zero_edge

    @pl.when(blk == B - 1)
    def _():
        TOPS[S : 2 * S] = zero_edge

    @pl.when(me == 0)
    def _():
        CR[0] = zero_block

    @pl.when(me == BS - 1)
    def _():
        CR[1] = zero_block

    outer = lev * (L + 1)
    for t in range(2):
        for b in range(NBD):
            X[t, outer, b] = zero_block

    load.wait()
    my_top = sub
    my_bot = S + sub

    def pack(k, packed):
        first, last = packed
        lanes = pl.ds(pl.multiple_of(k * CC, CC), CC)
        for t in range(2):
            for b in range(NBD):
                TOPS[my_top, t * NBD + b : t * NBD + b + 1, lanes] = X[t, k + 1, b, 0:1, :]
                BOTS[my_bot, t * NBD + b : t * NBD + b + 1, lanes] = X[t, k + 1, b, RC - 1 : RC, :]
            spot = t * L + k
            mine = lax.shift_right_logical(lane, 1) == spot
            first = jnp.where(mine, pltpu.roll(X[t, k + 1, 0], 2 * spot + 1, 1), first)
            last = jnp.where(mine, pltpu.roll(X[t, k + 1, NBD - 1], 2 * spot + 1, 1), last)
        return first, last

    many = 5 if L % 5 == 0 else 1

    def pack_many(i, packed):
        for j in range(many):
            packed = pack(i * many + j, packed)
        return packed

    first, last = lax.fori_loop(0, L // many, pack_many, (zero_block, zero_block))
    CP[0] = first
    CP[1] = last

    pl.semaphore_wait(barrier, BS)

    def top_slot(i):
        return TOPS.at[i]

    def bot_slot(i):
        return BOTS.at[i]

    def bot_to(i):
        return remote(
            bot_slot(S + sub), bot_slot(sub + (S if i < S else 0)), bot_s.at[i],
            bot_r.at[sub + (S if i < S else 0)],
            {"blk": blk + (0 if i < S else 1), "sub": i % S, "lev": lev},
        )

    def top_to(i):
        return remote(
            top_slot(sub), top_slot(sub + (0 if i < S else S)), top_s.at[i],
            top_r.at[sub + (0 if i < S else S)],
            {"blk": blk - (0 if i < S else 1), "sub": i % S, "lev": lev},
        )

    def each_edge(act):
        for i in range(S, 2 * S):
            pl.when(blk < B - 1)(lambda i=i: act(bot_to(i)))
            pl.when(blk > 0)(lambda i=i: act(top_to(i)))
        for i in range(S):
            pl.when(sub != i)(lambda i=i: act(bot_to(i)))
            pl.when(sub != i)(lambda i=i: act(top_to(i)))

    def col_down():
        return remote(CP.at[0], CR.at[1], col_s.at[0], col_r.at[1], at_dev(jnp.maximum(me - 1, 0)))

    def col_up():
        return remote(CP.at[1], CR.at[0], col_s.at[1], col_r.at[0], at_dev(jnp.minimum(me + 1, BS - 1)))

    each_edge(lambda c: c.start())
    pl.when(me > 0)(lambda: col_down().start())
    pl.when(me < BS - 1)(lambda: col_up().start())

    level_copy = remote(
        tr.at[:, pl.ds(other * (L - 1), 1)],
        X.at[:, pl.ds(lev * (L + 1), 1)],
        lev_sem.at[0], lev_sem.at[1], to_core,
    )
    level_copy.start()

    def m_to(d):
        dev = (me + d) % BS
        return remote(M.at[me, lev], M.at[me, lev], m_s.at[dev], m_r.at[me], at_dev(dev))

    def m_from(d):
        dev = (me + d) % BS
        return remote(M.at[dev, lev], M.at[dev, lev], m_s.at[dev], m_r.at[dev], at_dev(dev))

    @pl.loop(1, BS)
    def _(d):
        m_to(d).start()

    n8 = lax.broadcasted_iota(jnp.int32, (R8, 2 * S * R8), 0)
    c8 = lax.broadcasted_iota(jnp.int32, (R8, 2 * S * R8), 1)
    nba = jnp.zeros((R8, 2 * S * R8), jnp.int32)
    nbb = jnp.zeros((R8, 2 * S * R8), jnp.int32)
    for b in range(NBD):
        nba = jnp.where(n8 % NBD == b, nb[b, 0], nba)
        nbb = jnp.where(n8 % NBD == b, nb[b, 1], nbb)
    same_t = (n8 // NBD) == ((c8 // NBD) % 2)
    place = (c8 // R8) * NBD + c8 % NBD
    base = blk * S * NBD
    sel_a = jnp.where(same_t & (nba == place + base - S * NBD), 1.0, 0.0)
    sel_b = jnp.where(same_t & (nbb == place + base), 1.0, 0.0)

    for i in range(S):
        pl.when(blk > 0)(lambda i=i: remote(bot_slot(i), bot_slot(i), bot_s.at[i], bot_r.at[i], to_core).wait_recv())
        pl.when(sub != i)(
            lambda i=i: remote(bot_slot(S + i), bot_slot(S + i), bot_s.at[i], bot_r.at[S + i], to_core).wait_recv()
        )
        pl.when(sub != i)(lambda i=i: remote(top_slot(i), top_slot(i), top_s.at[i], top_r.at[i], to_core).wait_recv())
        pl.when(blk < B - 1)(
            lambda i=i: remote(top_slot(S + i), top_slot(S + i), top_s.at[i], top_r.at[S + i], to_core).wait_recv()
        )
    pl.when(me > 0)(lambda: remote(CR.at[0], CR.at[0], col_s.at[0], col_r.at[0], to_core).wait_recv())
    pl.when(me < BS - 1)(lambda: remote(CR.at[1], CR.at[1], col_s.at[1], col_r.at[1], to_core).wait_recv())
    level_copy.wait_recv()

    picked_a = jnp.dot(sel_a, BOTS[...].reshape(2 * S * R8, L * CC), precision=HIGH, preferred_element_type=F32)
    picked_b = jnp.dot(sel_b, TOPS[...].reshape(2 * S * R8, L * CC), precision=HIGH, preferred_element_type=F32)
    w8 = lax.broadcasted_iota(jnp.int32, (R8, L * CC), 0)
    open_a = jnp.zeros((R8, L * CC), jnp.int32)
    open_b = jnp.zeros((R8, L * CC), jnp.int32)
    for b in range(NBD):
        open_a = jnp.where(w8 % NBD == b, nb[b, 0], open_a)
        open_b = jnp.where(w8 % NBD == b, nb[b, 1], open_b)
    HA[...] = jnp.where(open_a < 0, TOPS[my_top], picked_a)
    HB[...] = jnp.where(open_b < 0, BOTS[my_bot], picked_b)

    wests = [jnp.full((RC, CC), nb[b, 2], jnp.int32) for b in range(NBD)]
    easts = [jnp.full((RC, CC), nb[b, 3], jnp.int32) for b in range(NBD)]
    levels = lt.shape[0]

    def step(k, cols):
        lanes = pl.ds(pl.multiple_of(k * CC, CC), CC)
        g = lev * L + k
        above = jnp.where(g == 0, 0.0, vm[jnp.maximum(g - 1, 0)])
        below = jnp.where(g == levels - 1, 0.0, vm[jnp.minimum(g, levels - 2)])
        thick = lt[g]
        new = []
        ends = []
        for t in range(2):
            shift = CC - 1 - 2 * (t * L + k)
            ends.append((pltpu.roll(CR[0], shift, 1), pltpu.roll(CR[1], shift, 1)))
        for b in range(NBD):
            q = me * NBD + b
            nxt = []
            for t in range(2):
                v = X[t, k + 1, b]
                before = ends[t][0] if b == 0 else X[t, k + 1, b - 1]
                after = ends[t][1] if b == NBD - 1 else X[t, k + 1, b + 1]
                spread = five_point(
                    v, before, after, HA[t * NBD + b : t * NBD + b + 1, lanes],
                    HB[t * NBD + b : t * NBD + b + 1, lanes], wests[b], easts[b], q, row, lane,
                )
                vertical = below * (X[t, k + 2, b] - v) - above * (v - X[t, k, b])
                y = v + hd[b] * spread + vertical
                Y[t, k, b] = y
                nxt.append(y)
            weighted = thick * (0.6 * nxt[0] + 0.05 * nxt[0] * nxt[0] - 0.8 * nxt[1])
            col = cols[b] + weighted
            C[k, b] = col
            new.append(col)
        return tuple(new)

    totals = lax.fori_loop(0, L, step, (zero_block,) * NBD)
    for b in range(NBD):
        TOT[b] = totals[b]
    tot_copy = remote(TOT, TIN, core_s.at[0], core_r.at[0], to_core)
    tot_copy.start()

    tot_copy.wait_recv()
    for b in range(NBD):
        G[me, b // H, b % H] = TOT[b] + TIN[b]

    def g_to(d):
        dev = (me + d) % BS
        return remote(G.at[me, lev], G.at[me, lev], g_s.at[dev], g_r.at[me], at_dev(dev))

    def g_from(d):
        dev = (me + d) % BS
        return remote(G.at[dev, lev], G.at[dev, lev], g_s.at[dev], g_r.at[dev], at_dev(dev))

    @pl.loop(1, BS)
    def _(d):
        g_to(d).start()

    @pl.loop(1, BS)
    def _(d):
        m_from(d).wait_recv()

    m_core = remote(M.at[:, lev], M.at[:, lev], core_s.at[1], core_r.at[1], to_core)
    m_core.start()

    remote(M.at[:, other], M.at[:, other], core_s.at[1], core_r.at[1], to_core).wait_recv()

    @pl.loop(0, BS)
    def _(d):
        for l in range(2):
            NBI[pl.ds(pl.multiple_of(d * NBD * 4 + l * H * 4, 8), H * 4), :] = M[
                d, l, MR : MR + H * 4, :
            ].astype(jnp.int32)

    KP = T.shape[0]
    PA[...] = NBI[pl.ds(0, NR, stride=4), :]
    PB[...] = NBI[pl.ds(1, NR, stride=4), :]
    wide = lax.broadcasted_iota(jnp.int32, (NR, CC), 1)
    for c in range(KP // CC):
        QA[:, c * CC : (c + 1) * CC] = jnp.where(PA[...] == wide + c * CC, 1.0, 0.0)
        QB[:, c * CC : (c + 1) * CC] = jnp.where(PB[...] == wide + c * CC, 1.0, 0.0)
    if KP > NR:
        T[NR:KP, :] = jnp.zeros((KP - NR, CC), F32)
        BT[NR:KP, :] = jnp.zeros((KP - NR, CC), F32)
    D[0] = zero_block
    D[NR + 1] = zero_block

    def over_core(d, l):
        dev = (me + d) % BS
        return remote(G.at[dev, l], G.at[dev, l], gc_s.at[dev], gc_r.at[dev], to_core)

    @pl.loop(1, BS)
    def _(d):
        g_from(d).wait_recv()
        over_core(d, lev).start()

    @pl.loop(1, BS)
    def _(d):
        over_core(d, other).wait_recv()

    @pl.loop(1, BS)
    def _(d):
        g_to(d).wait_send()
        over_core(d, lev).wait_send()

    def total(acc):
        return jnp.sum(jnp.sum(acc, axis=0, keepdims=True), axis=1, keepdims=True)

    def over_blocks(body, carry):
        pair = 2 if BS % 2 == 0 else 1

        def devs(i, carry):
            for p in range(pair):
                d = i * pair + p
                for b in range(NBD):
                    carry = body(d, b, d * NBD + b, carry)
            return carry

        return lax.fori_loop(0, BS // pair, devs, carry)

    def set_direction(q, d):
        D[q + 1] = d
        T[pl.ds(q, 1), :] = d[0:1, :]
        BT[pl.ds(q, 1), :] = d[RC - 1 : RC, :]

    def begin(d, b, q, acc):
        f = G[d, b // H, b % H]
        set_direction(q, f)
        return acc + f * f

    norm_now = total(over_blocks(begin, zero_block))
    wanted = [me * NBD + b for b in range(NBD)]
    wanted += [jnp.maximum(baro[s], 0) for s in range(baro.shape[0])]
    eta = [zero_block] * len(wanted)
    for iteration in range(ITERS):
        tops, bots = T[...], BT[...]
        up_rows = jnp.dot(QA[...], bots, precision=HIGH, preferred_element_type=F32)
        down_rows = jnp.dot(QB[...], tops, precision=HIGH, preferred_element_type=F32)
        HA2 = jnp.where(PA[...] < 0, T[0:NR, :], up_rows)
        HB2 = jnp.where(PB[...] < 0, BT[0:NR, :], down_rows)
        T[0:NR, :] = HA2
        BT[0:NR, :] = HB2

        def apply(d, b, q, acc):
            v = D[q + 1]
            west = jnp.broadcast_to(NBI[pl.ds(q * 4 + 2, 1), :], (RC, CC))
            east = jnp.broadcast_to(NBI[pl.ds(q * 4 + 3, 1), :], (RC, CC))
            spread = five_point(
                v, D[q], D[q + 2], T[pl.ds(q, 1), :], BT[pl.ds(q, 1), :], west, east, q, row, lane
            )
            diag = M[d, b // H, (b % H) * RC : (b % H + 1) * RC, :]
            applied = diag * v - spread
            AP[q] = applied
            return acc + v * applied

        size = norm_now / total(over_blocks(apply, zero_block))

        eta = [e + size * D[q + 1] for e, q in zip(eta, wanted)]
        if iteration == ITERS - 1:
            break

        def update(d, b, q, acc):
            r = G[d, b // H, b % H] - size * AP[q]
            G[d, b // H, b % H] = r
            return acc + r * r

        norm_next = total(over_blocks(update, zero_block))
        beta = norm_next / norm_now

        def turn(d, b, q, acc):
            set_direction(q, G[d, b // H, b % H] + beta * D[q + 1])
            return acc

        over_blocks(turn, jnp.int32(0))
        norm_now = norm_next

    levf = lev.astype(F32)
    raised = [eta[b] - levf * TIN[b] for b in range(NBD)]

    def press(k, _):
        for b in range(NBD):
            C[k, b] = raised[b] - C[k, b]
        return 0

    lax.fori_loop(0, L, press, 0)
    for s in range(baro.shape[0]):
        held = baro[s]
        out_s[s] = jnp.where(jnp.full((RC, CC), held, jnp.int32) >= 0, eta[NBD + s], 0.0)

    level_copy.wait_send()
    each_edge(lambda c: c.wait_send())
    pl.when(me > 0)(lambda: col_down().wait_send())
    pl.when(me < BS - 1)(lambda: col_up().wait_send())

    @pl.loop(1, BS)
    def _(d):
        m_to(d).wait_send()

    tot_copy.wait_send()
    m_core.wait_send()


def local(tracers, horizontal_diffusivity, vertical_mixing, layer_thickness, surface_diagonal, neighbours, baro_blocks):
    B, S = lax.axis_size("blk"), lax.axis_size("sub")
    L, NBD, RC, CC = tracers.shape[1:]
    BS = B * S
    NR = BS * NBD
    H = NBD // 2
    R8 = 2 * NBD
    KP = -(-NR // CC) * CC
    vm = pltpu.VMEM
    dma = pltpu.SemaphoreType.DMA
    slots = baro_blocks.shape[0]
    smem = pltpu.SMEM
    scratch = [
        vm((NBD, RC, CC), F32),
        smem(vertical_mixing.shape, F32),
        smem(layer_thickness.shape, F32),
        vm((NBD, RC, CC), F32),
        smem(neighbours.shape, jnp.int32),
        smem(baro_blocks.shape, jnp.int32),
        vm((2, L + 2, NBD, RC, CC), F32),
        vm((2 * S, R8, L * CC), F32),
        vm((2 * S, R8, L * CC), F32),
        vm((R8, L * CC), F32),
        vm((R8, L * CC), F32),
        vm((2, RC, CC), F32),
        vm((2, RC, CC), F32),
        vm((NBD, RC, CC), F32),
        vm((NBD, RC, CC), F32),
        vm((BS, 2, H * RC + H * 4, CC), F32),
        vm((NR * 4, CC), jnp.int32),
        vm((BS, 2, H, RC, CC), F32),
        vm((NR + 2, RC, CC), F32),
        vm((NR, RC, CC), F32),
        vm((KP, CC), F32),
        vm((KP, CC), F32),
        vm((NR, CC), jnp.int32),
        vm((NR, CC), jnp.int32),
        vm((NR, KP), F32),
        vm((NR, KP), F32),
        dma((7,)), dma((2,)), dma((2 * S,)), dma((2 * S,)), dma((2 * S,)), dma((2 * S,)),
        dma((2,)), dma((2,)), dma((BS,)), dma((BS,)), dma((BS,)), dma((BS,)), dma((BS,)), dma((BS,)), dma((2,)), dma((2,)),
    ]
    need = (10 * L * NBD + 7 * NR) * RC * CC * 4 + 4 * NR * KP * 4 + (8 << 20)
    vmem = pl.BlockSpec(memory_space=pltpu.VMEM)
    hbm = pl.BlockSpec(memory_space=pltpu.HBM)
    shapes = (
        jax.ShapeDtypeStruct(tracers.shape, F32),
        jax.ShapeDtypeStruct((L, NBD, RC, CC), F32),
        jax.ShapeDtypeStruct((slots, RC, CC), F32),
    )
    results = pl.pallas_call(
        functools.partial(kernel, B, S, (L, NBD, RC, CC)),
        out_shape=shapes,
        in_specs=[hbm] * 7,
        out_specs=(vmem,) * 3,
        scratch_shapes=scratch,
        compiler_params=pltpu.CompilerParams(
            collective_id=0, has_side_effects=True, vmem_limit_bytes=need
        ),
    )(*[
        pltpu.with_memory_space_constraint(x, pltpu.HBM)
        for x in (
            tracers, horizontal_diffusivity, vertical_mixing, layer_thickness, surface_diagonal,
            neighbours, baro_blocks,
        )
    ])
    return pl.pallas_call(
        write_out,
        out_shape=shapes,
        in_specs=[vmem] * 3,
        out_specs=(hbm,) * 3,
        scratch_shapes=[dma((4,))],
        compiler_params=pltpu.CompilerParams(vmem_limit_bytes=8 << 20),
    )(*results)


def write_out(tr, p, s, out_tr, out_p, out_s, sem):
    copies = [
        pltpu.make_async_copy(tr.at[0], out_tr.at[0], sem.at[0]),
        pltpu.make_async_copy(tr.at[1], out_tr.at[1], sem.at[1]),
        pltpu.make_async_copy(p, out_p, sem.at[2]),
        pltpu.make_async_copy(s, out_s, sem.at[3]),
    ]
    for copy in copies:
        copy.start()
    for copy in copies:
        copy.wait()


def solution(mesh):
    placed = (
        P("grp", "lev", ("blk", "sub"), None, None),
        P(("blk", "sub"), None, None),
        P(),
        P(),
        P(("blk", "sub"), None, None),
        P(("blk", "sub"), None),
        P(("blk", "sub", "lev")),
    )
    return jax.shard_map(
        local,
        mesh=mesh,
        in_specs=placed,
        out_specs=(
            P("grp", "lev", ("blk", "sub"), None, None),
            P(("grp", "lev"), ("blk", "sub"), None, None),
            P(("grp", "blk", "sub", "lev"), None, None),
        ),
        check_vma=False,
    )
```

```python
import functools

import jax
import jax.numpy as jnp
from jax import lax
from jax.experimental import pallas as pl
from jax.experimental.pallas import tpu as pltpu
from jax.sharding import PartitionSpec as P

ITERS = 3
F32 = jnp.float32
HIGH = lax.Precision.HIGHEST


def five_point(v, before, after, up, down, west, east, q, row, lane):
    rows, cols = v.shape
    xw = jnp.where(lane == cols - 1, jnp.where(west == q - 1, before, after), v)
    xe = jnp.where(lane == 0, jnp.where(east == q - 1, before, after), v)
    dw = jnp.where((lane == 0) & (west < 0), 0.0, pltpu.roll(xw, 1, 1) - v)
    de = jnp.where((lane == cols - 1) & (east < 0), 0.0, pltpu.roll(xe, cols - 1, 1) - v)
    fa = jnp.where(row == 0, jnp.broadcast_to(up, v.shape), pltpu.roll(v, 1, 0))
    fb = jnp.where(row == rows - 1, jnp.broadcast_to(down, v.shape), pltpu.roll(v, rows - 1, 0))
    return (fa - v) + (fb - v) + dw + de


def kernel(
    B, S, ITEMS,
    tr, hd_in, vm_in, lt_in, sd_in, nb_in, baro_in,
    Y, C, out_s,
    hd, vm, lt, sd, nb, baro, X, TOPS, BOTS, HA, HB, CP, CR, TOT, TIN, M, NBI, G, D, AP, T, BT, PA, PB, QA, QB,
    loc, lev_sem, bot_s, bot_r, top_s, top_r, col_s, col_r, m_s, m_r, g_s, g_r, gc_s, gc_r, core_s, core_r,
):
    L, NBD, RC, CC = ITEMS
    BS = B * S
    NR = BS * NBD
    H = NBD // 2
    R8 = 2 * NBD
    blk, sub, lev = lax.axis_index("blk"), lax.axis_index("sub"), lax.axis_index("lev")
    me = blk * S + sub
    other = 1 - lev
    row = lax.broadcasted_iota(jnp.int32, (RC, CC), 0)
    lane = lax.broadcasted_iota(jnp.int32, (RC, CC), 1)

    def at_dev(d):
        return {"blk": d // S, "sub": d % S, "lev": lev}

    load = pltpu.make_async_copy(tr, X.at[:, 1 : L + 1], loc.at[0])
    load.start()
    small = [
        pltpu.make_async_copy(source, target, loc.at[1 + i])
        for i, (source, target) in enumerate(
            [(nb_in, nb), (sd_in, sd), (hd_in, hd), (vm_in, vm), (lt_in, lt), (baro_in, baro)]
        )
    ]
    for copy in small:
        copy.start()

    barrier = pltpu.get_barrier_semaphore()
    pl.semaphore_signal(barrier, inc=1, device_id={"lev": other}, device_id_type=pl.DeviceIdType.MESH)

    @pl.loop(1, BS)
    def _(d):
        pl.semaphore_signal(
            barrier, inc=1, device_id=at_dev((me + d) % BS), device_id_type=pl.DeviceIdType.MESH
        )


    def remote(src, dst, ss, rs, dev):
        return pltpu.make_async_remote_copy(
            src_ref=src, dst_ref=dst, send_sem=ss, recv_sem=rs, device_id=dev,
            device_id_type=pl.DeviceIdType.MESH,
        )

    to_core = {"lev": other}
    for copy in small:
        copy.wait()
    MR = H * RC
    for j in range(H):
        M[me, lev, j * RC : (j + 1) * RC, :] = sd[lev * H + j]
    r8 = lax.broadcasted_iota(jnp.int32, (H * 4, CC), 0)
    lists = jnp.zeros((H * 4, CC), jnp.int32)
    for j in range(H):
        for s in range(4):
            lists = jnp.where(r8 == j * 4 + s, nb[lev * H + j, s], lists)
    M[me, lev, MR : MR + H * 4, :] = lists.astype(F32)

    zero_edge = jnp.zeros((S, R8, L * CC), F32)
    zero_block = jnp.zeros((RC, CC), F32)

    @pl.when(blk == 0)
    def _():
        BOTS[0:S] = zero_edge

    @pl.when(blk == B - 1)
    def _():
        TOPS[S : 2 * S] = zero_edge

    @pl.when(me == 0)
    def _():
        CR[0] = zero_block

    @pl.when(me == BS - 1)
    def _():
        CR[1] = zero_block

    outer = lev * (L + 1)
    for t in range(2):
        for b in range(NBD):
            X[t, outer, b] = zero_block

    load.wait()
    my_top = sub
    my_bot = S + sub

    def pack(k, packed):
        first, last = packed
        lanes = pl.ds(pl.multiple_of(k * CC, CC), CC)
        for t in range(2):
            for b in range(NBD):
                TOPS[my_top, t * NBD + b : t * NBD + b + 1, lanes] = X[t, k + 1, b, 0:1, :]
                BOTS[my_bot, t * NBD + b : t * NBD + b + 1, lanes] = X[t, k + 1, b, RC - 1 : RC, :]
            spot = t * L + k
            mine = lax.shift_right_logical(lane, 1) == spot
            first = jnp.where(mine, pltpu.roll(X[t, k + 1, 0], 2 * spot + 1, 1), first)
            last = jnp.where(mine, pltpu.roll(X[t, k + 1, NBD - 1], 2 * spot + 1, 1), last)
        return first, last

    many = 5 if L % 5 == 0 else 1

    def pack_many(i, packed):
        for j in range(many):
            packed = pack(i * many + j, packed)
        return packed

    first, last = lax.fori_loop(0, L // many, pack_many, (zero_block, zero_block))
    CP[0] = first
    CP[1] = last

    pl.semaphore_wait(barrier, BS)

    def top_slot(i):
        return TOPS.at[i]

    def bot_slot(i):
        return BOTS.at[i]

    def bot_to(i):
        return remote(
            bot_slot(S + sub), bot_slot(sub + (S if i < S else 0)), bot_s.at[i],
            bot_r.at[sub + (S if i < S else 0)],
            {"blk": blk + (0 if i < S else 1), "sub": i % S, "lev": lev},
        )

    def top_to(i):
        return remote(
            top_slot(sub), top_slot(sub + (0 if i < S else S)), top_s.at[i],
            top_r.at[sub + (0 if i < S else S)],
            {"blk": blk - (0 if i < S else 1), "sub": i % S, "lev": lev},
        )

    def each_edge(act):
        for i in range(S, 2 * S):
            pl.when(blk < B - 1)(lambda i=i: act(bot_to(i)))
            pl.when(blk > 0)(lambda i=i: act(top_to(i)))
        for i in range(S):
            pl.when(sub != i)(lambda i=i: act(bot_to(i)))
            pl.when(sub != i)(lambda i=i: act(top_to(i)))

    def col_down():
        return remote(CP.at[0], CR.at[1], col_s.at[0], col_r.at[1], at_dev(jnp.maximum(me - 1, 0)))

    def col_up():
        return remote(CP.at[1], CR.at[0], col_s.at[1], col_r.at[0], at_dev(jnp.minimum(me + 1, BS - 1)))

    each_edge(lambda c: c.start())
    pl.when(me > 0)(lambda: col_down().start())
    pl.when(me < BS - 1)(lambda: col_up().start())

    level_copy = remote(
        tr.at[:, pl.ds(other * (L - 1), 1)],
        X.at[:, pl.ds(lev * (L + 1), 1)],
        lev_sem.at[0], lev_sem.at[1], to_core,
    )
    level_copy.start()

    def pass_piece(buf, send, recv, p, target):
        return remote(buf.at[p, lev], buf.at[p, lev], send.at[target], recv.at[p], at_dev(target))

    def along_blk(buf, send, recv, e):
        target = ((blk + e) % B) * S + sub
        return pass_piece(buf, send, recv, me, target)

    def along_sub(buf, send, recv, e, f):
        other_blk = (blk + e) % B
        u = (sub + f) % S
        p = other_blk * S + sub
        return remote(
            buf.at[p, lev], buf.at[p, lev], send.at[other_blk * S + u], recv.at[p],
            at_dev(blk * S + u),
        )

    def arrive(buf, send, recv, e, f):
        p = ((blk + e) % B) * S + (sub + f) % S
        remote(buf.at[p, lev], buf.at[p, lev], send.at[p], recv.at[p], to_core).wait_recv()

    def each_sub(act):
        for f in range(1, S):
            act(f)

    @pl.loop(1, B)
    def _(e):
        along_blk(M, m_s, m_r, e).start()

    each_sub(lambda f: along_sub(M, m_s, m_r, 0, f).start())

    n8 = lax.broadcasted_iota(jnp.int32, (R8, 2 * S * R8), 0)
    c8 = lax.broadcasted_iota(jnp.int32, (R8, 2 * S * R8), 1)
    nba = jnp.zeros((R8, 2 * S * R8), jnp.int32)
    nbb = jnp.zeros((R8, 2 * S * R8), jnp.int32)
    for b in range(NBD):
        nba = jnp.where(n8 % NBD == b, nb[b, 0], nba)
        nbb = jnp.where(n8 % NBD == b, nb[b, 1], nbb)
    same_t = (n8 // NBD) == ((c8 // NBD) % 2)
    place = (c8 // R8) * NBD + c8 % NBD
    base = blk * S * NBD
    sel_a = jnp.where(same_t & (nba == place + base - S * NBD), 1.0, 0.0)
    sel_b = jnp.where(same_t & (nbb == place + base), 1.0, 0.0)

    for i in range(S):
        pl.when(blk > 0)(lambda i=i: remote(bot_slot(i), bot_slot(i), bot_s.at[i], bot_r.at[i], to_core).wait_recv())
        pl.when(sub != i)(
            lambda i=i: remote(bot_slot(S + i), bot_slot(S + i), bot_s.at[i], bot_r.at[S + i], to_core).wait_recv()
        )
        pl.when(sub != i)(lambda i=i: remote(top_slot(i), top_slot(i), top_s.at[i], top_r.at[i], to_core).wait_recv())
        pl.when(blk < B - 1)(
            lambda i=i: remote(top_slot(S + i), top_slot(S + i), top_s.at[i], top_r.at[S + i], to_core).wait_recv()
        )
    pl.when(me > 0)(lambda: remote(CR.at[0], CR.at[0], col_s.at[0], col_r.at[0], to_core).wait_recv())
    pl.when(me < BS - 1)(lambda: remote(CR.at[1], CR.at[1], col_s.at[1], col_r.at[1], to_core).wait_recv())
    level_copy.wait_recv()

    picked_a = jnp.dot(sel_a, BOTS[...].reshape(2 * S * R8, L * CC), precision=HIGH, preferred_element_type=F32)
    picked_b = jnp.dot(sel_b, TOPS[...].reshape(2 * S * R8, L * CC), precision=HIGH, preferred_element_type=F32)
    w8 = lax.broadcasted_iota(jnp.int32, (R8, L * CC), 0)
    open_a = jnp.zeros((R8, L * CC), jnp.int32)
    open_b = jnp.zeros((R8, L * CC), jnp.int32)
    for b in range(NBD):
        open_a = jnp.where(w8 % NBD == b, nb[b, 0], open_a)
        open_b = jnp.where(w8 % NBD == b, nb[b, 1], open_b)
    HA[...] = jnp.where(open_a < 0, TOPS[my_top], picked_a)
    HB[...] = jnp.where(open_b < 0, BOTS[my_bot], picked_b)

    wests = [jnp.full((RC, CC), nb[b, 2], jnp.int32) for b in range(NBD)]
    easts = [jnp.full((RC, CC), nb[b, 3], jnp.int32) for b in range(NBD)]
    levels = lt.shape[0]

    def step(k, cols):
        lanes = pl.ds(pl.multiple_of(k * CC, CC), CC)
        g = lev * L + k
        above = jnp.where(g == 0, 0.0, vm[jnp.maximum(g - 1, 0)])
        below = jnp.where(g == levels - 1, 0.0, vm[jnp.minimum(g, levels - 2)])
        thick = lt[g]
        new = []
        ends = []
        for t in range(2):
            shift = CC - 1 - 2 * (t * L + k)
            ends.append((pltpu.roll(CR[0], shift, 1), pltpu.roll(CR[1], shift, 1)))
        for b in range(NBD):
            q = me * NBD + b
            nxt = []
            for t in range(2):
                v = X[t, k + 1, b]
                before = ends[t][0] if b == 0 else X[t, k + 1, b - 1]
                after = ends[t][1] if b == NBD - 1 else X[t, k + 1, b + 1]
                spread = five_point(
                    v, before, after, HA[t * NBD + b : t * NBD + b + 1, lanes],
                    HB[t * NBD + b : t * NBD + b + 1, lanes], wests[b], easts[b], q, row, lane,
                )
                vertical = below * (X[t, k + 2, b] - v) - above * (v - X[t, k, b])
                y = v + hd[b] * spread + vertical
                Y[t, k, b] = y
                nxt.append(y)
            weighted = thick * (0.6 * nxt[0] + 0.05 * nxt[0] * nxt[0] - 0.8 * nxt[1])
            col = cols[b] + weighted
            C[k, b] = col
            new.append(col)
        return tuple(new)

    totals = lax.fori_loop(0, L, step, (zero_block,) * NBD)
    for b in range(NBD):
        TOT[b] = totals[b]
    tot_copy = remote(TOT, TIN, core_s.at[0], core_r.at[0], to_core)
    tot_copy.start()

    @pl.loop(1, B)
    def _(e):
        arrive(M, m_s, m_r, e, 0)
        each_sub(lambda f: along_sub(M, m_s, m_r, e, f).start())


    tot_copy.wait_recv()
    for b in range(NBD):
        G[me, b // H, b % H] = TOT[b] + TIN[b]

    def over_core(e, f, l):
        p = ((blk + e) % B) * S + (sub + f) % S
        return remote(G.at[p, l], G.at[p, l], gc_s.at[p], gc_r.at[p], to_core)

    @pl.loop(1, B)
    def _(e):
        along_blk(G, g_s, g_r, e).start()

    each_sub(lambda f: along_sub(G, g_s, g_r, 0, f).start())

    @pl.loop(0, B)
    def _(e):
        each_sub(lambda f: arrive(M, m_s, m_r, e, f))

    m_core = remote(M.at[:, lev], M.at[:, lev], core_s.at[1], core_r.at[1], to_core)
    m_core.start()

    @pl.loop(1, B)
    def _(e):
        arrive(G, g_s, g_r, e, 0)
        each_sub(lambda f: along_sub(G, g_s, g_r, e, f).start())
        over_core(e, 0, lev).start()

    remote(M.at[:, other], M.at[:, other], core_s.at[1], core_r.at[1], to_core).wait_recv()

    @pl.loop(0, BS)
    def _(d):
        for l in range(2):
            NBI[pl.ds(pl.multiple_of(d * NBD * 4 + l * H * 4, 8), H * 4), :] = M[
                d, l, MR : MR + H * 4, :
            ].astype(jnp.int32)

    KP = T.shape[0]
    PA[...] = NBI[pl.ds(0, NR, stride=4), :]
    PB[...] = NBI[pl.ds(1, NR, stride=4), :]
    wide = lax.broadcasted_iota(jnp.int32, (NR, CC), 1)
    for c in range(KP // CC):
        QA[:, c * CC : (c + 1) * CC] = jnp.where(PA[...] == wide + c * CC, 1.0, 0.0)
        QB[:, c * CC : (c + 1) * CC] = jnp.where(PB[...] == wide + c * CC, 1.0, 0.0)
    if KP > NR:
        T[NR:KP, :] = jnp.zeros((KP - NR, CC), F32)
        BT[NR:KP, :] = jnp.zeros((KP - NR, CC), F32)
    D[0] = zero_block
    D[NR + 1] = zero_block

    @pl.loop(0, B)
    def _(e):
        def take(f):
            arrive(G, g_s, g_r, e, f)
            over_core(e, f, lev).start()

        each_sub(take)

    @pl.loop(1, BS)
    def _(d):
        over_core(d // S, d % S, other).wait_recv()

    @pl.loop(1, B)
    def _(e):
        along_blk(G, g_s, g_r, e).wait_send()

    @pl.loop(0, B)
    def _(e):
        each_sub(lambda f: along_sub(G, g_s, g_r, e, f).wait_send())

    @pl.loop(1, BS)
    def _(d):
        over_core(d // S, d % S, lev).wait_send()

    def total(acc):
        return jnp.sum(jnp.sum(acc, axis=0, keepdims=True), axis=1, keepdims=True)

    def over_blocks(body, carry):
        pair = 2 if BS % 2 == 0 else 1

        def devs(i, carry):
            for p in range(pair):
                d = i * pair + p
                for b in range(NBD):
                    carry = body(d, b, d * NBD + b, carry)
            return carry

        return lax.fori_loop(0, BS // pair, devs, carry)

    def set_direction(q, d):
        D[q + 1] = d
        T[pl.ds(q, 1), :] = d[0:1, :]
        BT[pl.ds(q, 1), :] = d[RC - 1 : RC, :]

    def begin(d, b, q, acc):
        f = G[d, b // H, b % H]
        set_direction(q, f)
        return acc + f * f

    norm_now = total(over_blocks(begin, zero_block))
    wanted = [me * NBD + b for b in range(NBD)]
    wanted += [jnp.maximum(baro[s], 0) for s in range(baro.shape[0])]
    eta = [zero_block] * len(wanted)
    for iteration in range(ITERS):
        tops, bots = T[...], BT[...]
        up_rows = jnp.dot(QA[...], bots, precision=HIGH, preferred_element_type=F32)
        down_rows = jnp.dot(QB[...], tops, precision=HIGH, preferred_element_type=F32)
        HA2 = jnp.where(PA[...] < 0, T[0:NR, :], up_rows)
        HB2 = jnp.where(PB[...] < 0, BT[0:NR, :], down_rows)
        T[0:NR, :] = HA2
        BT[0:NR, :] = HB2

        def apply(d, b, q, acc):
            v = D[q + 1]
            west = jnp.broadcast_to(NBI[pl.ds(q * 4 + 2, 1), :], (RC, CC))
            east = jnp.broadcast_to(NBI[pl.ds(q * 4 + 3, 1), :], (RC, CC))
            spread = five_point(
                v, D[q], D[q + 2], T[pl.ds(q, 1), :], BT[pl.ds(q, 1), :], west, east, q, row, lane
            )
            diag = M[d, b // H, (b % H) * RC : (b % H + 1) * RC, :]
            applied = diag * v - spread
            AP[q] = applied
            return acc + v * applied

        size = norm_now / total(over_blocks(apply, zero_block))

        eta = [e + size * D[q + 1] for e, q in zip(eta, wanted)]
        if iteration == ITERS - 1:
            break

        def update(d, b, q, acc):
            r = G[d, b // H, b % H] - size * AP[q]
            G[d, b // H, b % H] = r
            return acc + r * r

        norm_next = total(over_blocks(update, zero_block))
        beta = norm_next / norm_now

        def turn(d, b, q, acc):
            set_direction(q, G[d, b // H, b % H] + beta * D[q + 1])
            return acc

        over_blocks(turn, jnp.int32(0))
        norm_now = norm_next

    levf = lev.astype(F32)
    raised = [eta[b] - levf * TIN[b] for b in range(NBD)]

    def press(k, _):
        for b in range(NBD):
            C[k, b] = raised[b] - C[k, b]
        return 0

    lax.fori_loop(0, L, press, 0)
    for s in range(baro.shape[0]):
        held = baro[s]
        out_s[s] = jnp.where(jnp.full((RC, CC), held, jnp.int32) >= 0, eta[NBD + s], 0.0)

    level_copy.wait_send()
    each_edge(lambda c: c.wait_send())
    pl.when(me > 0)(lambda: col_down().wait_send())
    pl.when(me < BS - 1)(lambda: col_up().wait_send())

    @pl.loop(1, B)
    def _(e):
        along_blk(M, m_s, m_r, e).wait_send()

    @pl.loop(0, B)
    def _(e):
        each_sub(lambda f: along_sub(M, m_s, m_r, e, f).wait_send())

    tot_copy.wait_send()
    m_core.wait_send()


def local(tracers, horizontal_diffusivity, vertical_mixing, layer_thickness, surface_diagonal, neighbours, baro_blocks):
    B, S = lax.axis_size("blk"), lax.axis_size("sub")
    L, NBD, RC, CC = tracers.shape[1:]
    BS = B * S
    NR = BS * NBD
    H = NBD // 2
    R8 = 2 * NBD
    KP = -(-NR // CC) * CC
    vm = pltpu.VMEM
    dma = pltpu.SemaphoreType.DMA
    slots = baro_blocks.shape[0]
    smem = pltpu.SMEM
    scratch = [
        vm((NBD, RC, CC), F32),
        smem(vertical_mixing.shape, F32),
        smem(layer_thickness.shape, F32),
        vm((NBD, RC, CC), F32),
        smem(neighbours.shape, jnp.int32),
        smem(baro_blocks.shape, jnp.int32),
        vm((2, L + 2, NBD, RC, CC), F32),
        vm((2 * S, R8, L * CC), F32),
        vm((2 * S, R8, L * CC), F32),
        vm((R8, L * CC), F32),
        vm((R8, L * CC), F32),
        vm((2, RC, CC), F32),
        vm((2, RC, CC), F32),
        vm((NBD, RC, CC), F32),
        vm((NBD, RC, CC), F32),
        vm((BS, 2, H * RC + H * 4, CC), F32),
        vm((NR * 4, CC), jnp.int32),
        vm((BS, 2, H, RC, CC), F32),
        vm((NR + 2, RC, CC), F32),
        vm((NR, RC, CC), F32),
        vm((KP, CC), F32),
        vm((KP, CC), F32),
        vm((NR, CC), jnp.int32),
        vm((NR, CC), jnp.int32),
        vm((NR, KP), F32),
        vm((NR, KP), F32),
        dma((7,)), dma((2,)), dma((2 * S,)), dma((2 * S,)), dma((2 * S,)), dma((2 * S,)),
        dma((2,)), dma((2,)), dma((BS,)), dma((BS,)), dma((BS,)), dma((BS,)), dma((BS,)), dma((BS,)), dma((2,)), dma((2,)),
    ]
    need = (10 * L * NBD + 7 * NR) * RC * CC * 4 + 4 * NR * KP * 4 + (8 << 20)
    vmem = pl.BlockSpec(memory_space=pltpu.VMEM)
    hbm = pl.BlockSpec(memory_space=pltpu.HBM)
    shapes = (
        jax.ShapeDtypeStruct(tracers.shape, F32),
        jax.ShapeDtypeStruct((L, NBD, RC, CC), F32),
        jax.ShapeDtypeStruct((slots, RC, CC), F32),
    )
    results = pl.pallas_call(
        functools.partial(kernel, B, S, (L, NBD, RC, CC)),
        out_shape=shapes,
        in_specs=[hbm] * 7,
        out_specs=(vmem,) * 3,
        scratch_shapes=scratch,
        compiler_params=pltpu.CompilerParams(
            collective_id=0, has_side_effects=True, vmem_limit_bytes=need
        ),
    )(*[
        pltpu.with_memory_space_constraint(x, pltpu.HBM)
        for x in (
            tracers, horizontal_diffusivity, vertical_mixing, layer_thickness, surface_diagonal,
            neighbours, baro_blocks,
        )
    ])
    return pl.pallas_call(
        write_out,
        out_shape=shapes,
        in_specs=[vmem] * 3,
        out_specs=(hbm,) * 3,
        scratch_shapes=[dma((4,))],
        compiler_params=pltpu.CompilerParams(vmem_limit_bytes=8 << 20),
    )(*results)


def write_out(tr, p, s, out_tr, out_p, out_s, sem):
    copies = [
        pltpu.make_async_copy(tr.at[0], out_tr.at[0], sem.at[0]),
        pltpu.make_async_copy(tr.at[1], out_tr.at[1], sem.at[1]),
        pltpu.make_async_copy(p, out_p, sem.at[2]),
        pltpu.make_async_copy(s, out_s, sem.at[3]),
    ]
    for copy in copies:
        copy.start()
    for copy in copies:
        copy.wait()


def solution(mesh):
    placed = (
        P("grp", "lev", ("blk", "sub"), None, None),
        P(("blk", "sub"), None, None),
        P(),
        P(),
        P(("blk", "sub"), None, None),
        P(("blk", "sub"), None),
        P(("blk", "sub", "lev")),
    )
    return jax.shard_map(
        local,
        mesh=mesh,
        in_specs=placed,
        out_specs=(
            P("grp", "lev", ("blk", "sub"), None, None),
            P(("grp", "lev"), ("blk", "sub"), None, None),
            P(("grp", "blk", "sub", "lev"), None, None),
        ),
        check_vma=False,
    )
```

```python
import functools

import jax
import jax.numpy as jnp
from jax import lax
from jax.experimental import pallas as pl
from jax.experimental.pallas import tpu as pltpu
from jax.sharding import PartitionSpec as P

ITERS = 3
F32 = jnp.float32
HIGH = lax.Precision.HIGHEST


def five_point(v, before, after, up, down, west, east, q, row, lane):
    rows, cols = v.shape
    xw = jnp.where(lane == cols - 1, jnp.where(west == q - 1, before, after), v)
    xe = jnp.where(lane == 0, jnp.where(east == q - 1, before, after), v)
    dw = jnp.where((lane == 0) & (west < 0), 0.0, pltpu.roll(xw, 1, 1) - v)
    de = jnp.where((lane == cols - 1) & (east < 0), 0.0, pltpu.roll(xe, cols - 1, 1) - v)
    fa = jnp.where(row == 0, jnp.broadcast_to(up, v.shape), pltpu.roll(v, 1, 0))
    fb = jnp.where(row == rows - 1, jnp.broadcast_to(down, v.shape), pltpu.roll(v, rows - 1, 0))
    return (fa - v) + (fb - v) + dw + de


def kernel(
    B, S, ITEMS,
    tr, hd_in, vm_in, lt_in, sd_in, nb_in, baro_in,
    Y, C, out_s,
    hd, vm, lt, sd, nb, baro, X, TOPS, BOTS, HA, HB, CP, CR, TOT, TIN, M, NBI, G, D, AP, T, BT, PA, PB, QA, QB,
    loc, lev_sem, bot_s, bot_r, top_s, top_r, col_s, col_r, m_s, m_r, g_s, g_r, gc_s, gc_r, core_s, core_r,
):
    L, NBD, RC, CC = ITEMS
    BS = B * S
    NR = BS * NBD
    H = NBD // 2
    R8 = 2 * NBD
    blk, sub, lev = lax.axis_index("blk"), lax.axis_index("sub"), lax.axis_index("lev")
    me = blk * S + sub
    other = 1 - lev
    row = lax.broadcasted_iota(jnp.int32, (RC, CC), 0)
    lane = lax.broadcasted_iota(jnp.int32, (RC, CC), 1)

    def at_dev(d):
        return {"blk": d // S, "sub": d % S, "lev": lev}

    load = pltpu.make_async_copy(tr, X.at[:, 1 : L + 1], loc.at[0])
    load.start()
    small = [
        pltpu.make_async_copy(source, target, loc.at[1 + i])
        for i, (source, target) in enumerate(
            [(nb_in, nb), (sd_in, sd), (hd_in, hd), (vm_in, vm), (lt_in, lt), (baro_in, baro)]
        )
    ]
    for copy in small:
        copy.start()

    barrier = pltpu.get_barrier_semaphore()
    pl.semaphore_signal(barrier, inc=1, device_id={"lev": other}, device_id_type=pl.DeviceIdType.MESH)

    @pl.loop(1, BS)
    def _(d):
        pl.semaphore_signal(
            barrier, inc=1, device_id=at_dev((me + d) % BS), device_id_type=pl.DeviceIdType.MESH
        )


    def remote(src, dst, ss, rs, dev):
        return pltpu.make_async_remote_copy(
            src_ref=src, dst_ref=dst, send_sem=ss, recv_sem=rs, device_id=dev,
            device_id_type=pl.DeviceIdType.MESH,
        )

    to_core = {"lev": other}
    for copy in small:
        copy.wait()
    MR = H * RC
    for j in range(H):
        M[me, lev, j * RC : (j + 1) * RC, :] = sd[lev * H + j]
    r8 = lax.broadcasted_iota(jnp.int32, (H * 4, CC), 0)
    lists = jnp.zeros((H * 4, CC), jnp.int32)
    for j in range(H):
        for s in range(4):
            lists = jnp.where(r8 == j * 4 + s, nb[lev * H + j, s], lists)
    M[me, lev, MR : MR + H * 4, :] = lists.astype(F32)

    zero_edge = jnp.zeros((S, R8, L * CC), F32)
    zero_block = jnp.zeros((RC, CC), F32)

    @pl.when(blk == 0)
    def _():
        BOTS[0:S] = zero_edge

    @pl.when(blk == B - 1)
    def _():
        TOPS[S : 2 * S] = zero_edge

    @pl.when(me == 0)
    def _():
        CR[0] = zero_block

    @pl.when(me == BS - 1)
    def _():
        CR[1] = zero_block

    outer = lev * (L + 1)
    for t in range(2):
        for b in range(NBD):
            X[t, outer, b] = zero_block

    load.wait()
    my_top = sub
    my_bot = S + sub

    def pack(k, packed):
        first, last = packed
        lanes = pl.ds(pl.multiple_of(k * CC, CC), CC)
        for t in range(2):
            for b in range(NBD):
                TOPS[my_top, t * NBD + b : t * NBD + b + 1, lanes] = X[t, k + 1, b, 0:1, :]
                BOTS[my_bot, t * NBD + b : t * NBD + b + 1, lanes] = X[t, k + 1, b, RC - 1 : RC, :]
            spot = t * L + k
            mine = lax.shift_right_logical(lane, 1) == spot
            first = jnp.where(mine, pltpu.roll(X[t, k + 1, 0], 2 * spot + 1, 1), first)
            last = jnp.where(mine, pltpu.roll(X[t, k + 1, NBD - 1], 2 * spot + 1, 1), last)
        return first, last

    many = 5 if L % 5 == 0 else 1

    def pack_many(i, packed):
        for j in range(many):
            packed = pack(i * many + j, packed)
        return packed

    first, last = lax.fori_loop(0, L // many, pack_many, (zero_block, zero_block))
    CP[0] = first
    CP[1] = last

    pl.semaphore_wait(barrier, BS)

    def top_slot(i):
        return TOPS.at[i]

    def bot_slot(i):
        return BOTS.at[i]

    def bot_to(i):
        return remote(
            bot_slot(S + sub), bot_slot(sub + (S if i < S else 0)), bot_s.at[i],
            bot_r.at[sub + (S if i < S else 0)],
            {"blk": blk + (0 if i < S else 1), "sub": i % S, "lev": lev},
        )

    def top_to(i):
        return remote(
            top_slot(sub), top_slot(sub + (0 if i < S else S)), top_s.at[i],
            top_r.at[sub + (0 if i < S else S)],
            {"blk": blk - (0 if i < S else 1), "sub": i % S, "lev": lev},
        )

    def each_edge(act):
        for i in range(S, 2 * S):
            pl.when(blk < B - 1)(lambda i=i: act(bot_to(i)))
            pl.when(blk > 0)(lambda i=i: act(top_to(i)))
        for i in range(S):
            pl.when(sub != i)(lambda i=i: act(bot_to(i)))
            pl.when(sub != i)(lambda i=i: act(top_to(i)))

    def col_down():
        return remote(CP.at[0], CR.at[1], col_s.at[0], col_r.at[1], at_dev(jnp.maximum(me - 1, 0)))

    def col_up():
        return remote(CP.at[1], CR.at[0], col_s.at[1], col_r.at[0], at_dev(jnp.minimum(me + 1, BS - 1)))

    each_edge(lambda c: c.start())
    pl.when(me > 0)(lambda: col_down().start())
    pl.when(me < BS - 1)(lambda: col_up().start())

    level_copy = remote(
        tr.at[:, pl.ds(other * (L - 1), 1)],
        X.at[:, pl.ds(lev * (L + 1), 1)],
        lev_sem.at[0], lev_sem.at[1], to_core,
    )
    level_copy.start()

    def m_to(d):
        dev = (me + d) % BS
        return remote(M.at[me, lev], M.at[me, lev], m_s.at[dev], m_r.at[me], at_dev(dev))

    def m_from(d):
        dev = (me + d) % BS
        return remote(M.at[dev, lev], M.at[dev, lev], m_s.at[dev], m_r.at[dev], at_dev(dev))

    @pl.loop(1, BS)
    def _(d):
        m_to(d).start()

    n8 = lax.broadcasted_iota(jnp.int32, (R8, 2 * S * R8), 0)
    c8 = lax.broadcasted_iota(jnp.int32, (R8, 2 * S * R8), 1)
    nba = jnp.zeros((R8, 2 * S * R8), jnp.int32)
    nbb = jnp.zeros((R8, 2 * S * R8), jnp.int32)
    for b in range(NBD):
        nba = jnp.where(n8 % NBD == b, nb[b, 0], nba)
        nbb = jnp.where(n8 % NBD == b, nb[b, 1], nbb)
    same_t = (n8 // NBD) == ((c8 // NBD) % 2)
    place = (c8 // R8) * NBD + c8 % NBD
    base = blk * S * NBD
    sel_a = jnp.where(same_t & (nba == place + base - S * NBD), 1.0, 0.0)
    sel_b = jnp.where(same_t & (nbb == place + base), 1.0, 0.0)

    for i in range(S):
        pl.when(blk > 0)(lambda i=i: remote(bot_slot(i), bot_slot(i), bot_s.at[i], bot_r.at[i], to_core).wait_recv())
        pl.when(sub != i)(
            lambda i=i: remote(bot_slot(S + i), bot_slot(S + i), bot_s.at[i], bot_r.at[S + i], to_core).wait_recv()
        )
        pl.when(sub != i)(lambda i=i: remote(top_slot(i), top_slot(i), top_s.at[i], top_r.at[i], to_core).wait_recv())
        pl.when(blk < B - 1)(
            lambda i=i: remote(top_slot(S + i), top_slot(S + i), top_s.at[i], top_r.at[S + i], to_core).wait_recv()
        )
    pl.when(me > 0)(lambda: remote(CR.at[0], CR.at[0], col_s.at[0], col_r.at[0], to_core).wait_recv())
    pl.when(me < BS - 1)(lambda: remote(CR.at[1], CR.at[1], col_s.at[1], col_r.at[1], to_core).wait_recv())
    level_copy.wait_recv()

    picked_a = jnp.dot(sel_a, BOTS[...].reshape(2 * S * R8, L * CC), precision=HIGH, preferred_element_type=F32)
    picked_b = jnp.dot(sel_b, TOPS[...].reshape(2 * S * R8, L * CC), precision=HIGH, preferred_element_type=F32)
    w8 = lax.broadcasted_iota(jnp.int32, (R8, L * CC), 0)
    open_a = jnp.zeros((R8, L * CC), jnp.int32)
    open_b = jnp.zeros((R8, L * CC), jnp.int32)
    for b in range(NBD):
        open_a = jnp.where(w8 % NBD == b, nb[b, 0], open_a)
        open_b = jnp.where(w8 % NBD == b, nb[b, 1], open_b)
    HA[...] = jnp.where(open_a < 0, TOPS[my_top], picked_a)
    HB[...] = jnp.where(open_b < 0, BOTS[my_bot], picked_b)

    wests = [jnp.full((RC, CC), nb[b, 2], jnp.int32) for b in range(NBD)]
    easts = [jnp.full((RC, CC), nb[b, 3], jnp.int32) for b in range(NBD)]
    levels = lt.shape[0]

    def step(k, cols):
        lanes = pl.ds(pl.multiple_of(k * CC, CC), CC)
        g = lev * L + k
        above = jnp.where(g == 0, 0.0, vm[jnp.maximum(g - 1, 0)])
        below = jnp.where(g == levels - 1, 0.0, vm[jnp.minimum(g, levels - 2)])
        thick = lt[g]
        new = []
        ends = []
        for t in range(2):
            shift = CC - 1 - 2 * (t * L + k)
            ends.append((pltpu.roll(CR[0], shift, 1), pltpu.roll(CR[1], shift, 1)))
        for b in range(NBD):
            q = me * NBD + b
            nxt = []
            for t in range(2):
                v = X[t, k + 1, b]
                before = ends[t][0] if b == 0 else X[t, k + 1, b - 1]
                after = ends[t][1] if b == NBD - 1 else X[t, k + 1, b + 1]
                spread = five_point(
                    v, before, after, HA[t * NBD + b : t * NBD + b + 1, lanes],
                    HB[t * NBD + b : t * NBD + b + 1, lanes], wests[b], easts[b], q, row, lane,
                )
                vertical = below * (X[t, k + 2, b] - v) - above * (v - X[t, k, b])
                y = v + hd[b] * spread + vertical
                Y[t, k, b] = y
                nxt.append(y)
            weighted = thick * (0.6 * nxt[0] + 0.05 * nxt[0] * nxt[0] - 0.8 * nxt[1])
            col = cols[b] + weighted
            C[k, b] = col
            new.append(col)
        return tuple(new)

    twice = 2 if L % 2 == 0 else 1

    def step_more(i, cols):
        for j in range(twice):
            cols = step(i * twice + j, cols)
        return cols

    totals = lax.fori_loop(0, L // twice, step_more, (zero_block,) * NBD)
    for b in range(NBD):
        TOT[b] = totals[b]
    tot_copy = remote(TOT, TIN, core_s.at[0], core_r.at[0], to_core)
    tot_copy.start()

    tot_copy.wait_recv()
    for b in range(NBD):
        G[me, b // H, b % H] = TOT[b] + TIN[b]

    def g_to(d):
        dev = (me + d) % BS
        return remote(G.at[me, lev], G.at[me, lev], g_s.at[dev], g_r.at[me], at_dev(dev))

    def g_from(d):
        dev = (me + d) % BS
        return remote(G.at[dev, lev], G.at[dev, lev], g_s.at[dev], g_r.at[dev], at_dev(dev))

    @pl.loop(1, BS)
    def _(d):
        g_to(d).start()

    @pl.loop(1, BS)
    def _(d):
        m_from(d).wait_recv()

    m_core = remote(M.at[:, lev], M.at[:, lev], core_s.at[1], core_r.at[1], to_core)
    m_core.start()

    remote(M.at[:, other], M.at[:, other], core_s.at[1], core_r.at[1], to_core).wait_recv()

    @pl.loop(0, BS)
    def _(d):
        for l in range(2):
            NBI[pl.ds(pl.multiple_of(d * NBD * 4 + l * H * 4, 8), H * 4), :] = M[
                d, l, MR : MR + H * 4, :
            ].astype(jnp.int32)

    KP = T.shape[0]
    PA[...] = NBI[pl.ds(0, NR, stride=4), :]
    PB[...] = NBI[pl.ds(1, NR, stride=4), :]
    wide = lax.broadcasted_iota(jnp.int32, (NR, CC), 1)
    for c in range(KP // CC):
        QA[:, c * CC : (c + 1) * CC] = jnp.where(PA[...] == wide + c * CC, 1.0, 0.0)
        QB[:, c * CC : (c + 1) * CC] = jnp.where(PB[...] == wide + c * CC, 1.0, 0.0)
    if KP > NR:
        T[NR:KP, :] = jnp.zeros((KP - NR, CC), F32)
        BT[NR:KP, :] = jnp.zeros((KP - NR, CC), F32)
    D[0] = zero_block
    D[NR + 1] = zero_block

    def over_core(d, l):
        dev = (me + d) % BS
        return remote(G.at[dev, l], G.at[dev, l], gc_s.at[dev], gc_r.at[dev], to_core)

    @pl.loop(1, BS)
    def _(d):
        g_from(d).wait_recv()
        over_core(d, lev).start()

    @pl.loop(1, BS)
    def _(d):
        over_core(d, other).wait_recv()

    @pl.loop(1, BS)
    def _(d):
        g_to(d).wait_send()
        over_core(d, lev).wait_send()

    def total(acc):
        return jnp.sum(jnp.sum(acc, axis=0, keepdims=True), axis=1, keepdims=True)

    def over_blocks(body, carry):
        pair = 4 if BS % 4 == 0 else 1

        def devs(i, carry):
            for p in range(pair):
                d = i * pair + p
                for b in range(NBD):
                    carry = body(d, b, d * NBD + b, carry)
            return carry

        return lax.fori_loop(0, BS // pair, devs, carry)

    def set_direction(q, d):
        D[q + 1] = d
        T[pl.ds(q, 1), :] = d[0:1, :]
        BT[pl.ds(q, 1), :] = d[RC - 1 : RC, :]

    def begin(d, b, q, acc):
        f = G[d, b // H, b % H]
        set_direction(q, f)
        return acc + f * f

    norm_now = total(over_blocks(begin, zero_block))
    wanted = [me * NBD + b for b in range(NBD)]
    wanted += [jnp.maximum(baro[s], 0) for s in range(baro.shape[0])]
    eta = [zero_block] * len(wanted)
    for iteration in range(ITERS):
        tops, bots = T[...], BT[...]
        up_rows = jnp.dot(QA[...], bots, precision=HIGH, preferred_element_type=F32)
        down_rows = jnp.dot(QB[...], tops, precision=HIGH, preferred_element_type=F32)
        HA2 = jnp.where(PA[...] < 0, T[0:NR, :], up_rows)
        HB2 = jnp.where(PB[...] < 0, BT[0:NR, :], down_rows)
        T[0:NR, :] = HA2
        BT[0:NR, :] = HB2

        def apply(d, b, q, acc):
            v = D[q + 1]
            west = jnp.broadcast_to(NBI[pl.ds(q * 4 + 2, 1), :], (RC, CC))
            east = jnp.broadcast_to(NBI[pl.ds(q * 4 + 3, 1), :], (RC, CC))
            spread = five_point(
                v, D[q], D[q + 2], T[pl.ds(q, 1), :], BT[pl.ds(q, 1), :], west, east, q, row, lane
            )
            diag = M[d, b // H, (b % H) * RC : (b % H + 1) * RC, :]
            applied = diag * v - spread
            AP[q] = applied
            return acc + v * applied

        size = norm_now / total(over_blocks(apply, zero_block))

        eta = [e + size * D[q + 1] for e, q in zip(eta, wanted)]
        if iteration == ITERS - 1:
            break

        def update(d, b, q, acc):
            r = G[d, b // H, b % H] - size * AP[q]
            G[d, b // H, b % H] = r
            return acc + r * r

        norm_next = total(over_blocks(update, zero_block))
        beta = norm_next / norm_now

        def turn(d, b, q, acc):
            set_direction(q, G[d, b // H, b % H] + beta * D[q + 1])
            return acc

        over_blocks(turn, jnp.int32(0))
        norm_now = norm_next

    levf = lev.astype(F32)
    raised = [eta[b] - levf * TIN[b] for b in range(NBD)]

    def press(k, _):
        for b in range(NBD):
            C[k, b] = raised[b] - C[k, b]
        return 0

    lax.fori_loop(0, L, press, 0)
    for s in range(baro.shape[0]):
        held = baro[s]
        out_s[s] = jnp.where(jnp.full((RC, CC), held, jnp.int32) >= 0, eta[NBD + s], 0.0)

    level_copy.wait_send()
    each_edge(lambda c: c.wait_send())
    pl.when(me > 0)(lambda: col_down().wait_send())
    pl.when(me < BS - 1)(lambda: col_up().wait_send())

    @pl.loop(1, BS)
    def _(d):
        m_to(d).wait_send()

    tot_copy.wait_send()
    m_core.wait_send()


def local(tracers, horizontal_diffusivity, vertical_mixing, layer_thickness, surface_diagonal, neighbours, baro_blocks):
    B, S = lax.axis_size("blk"), lax.axis_size("sub")
    L, NBD, RC, CC = tracers.shape[1:]
    BS = B * S
    NR = BS * NBD
    H = NBD // 2
    R8 = 2 * NBD
    KP = -(-NR // CC) * CC
    vm = pltpu.VMEM
    dma = pltpu.SemaphoreType.DMA
    slots = baro_blocks.shape[0]
    smem = pltpu.SMEM
    scratch = [
        vm((NBD, RC, CC), F32),
        smem(vertical_mixing.shape, F32),
        smem(layer_thickness.shape, F32),
        vm((NBD, RC, CC), F32),
        smem(neighbours.shape, jnp.int32),
        smem(baro_blocks.shape, jnp.int32),
        vm((2, L + 2, NBD, RC, CC), F32),
        vm((2 * S, R8, L * CC), F32),
        vm((2 * S, R8, L * CC), F32),
        vm((R8, L * CC), F32),
        vm((R8, L * CC), F32),
        vm((2, RC, CC), F32),
        vm((2, RC, CC), F32),
        vm((NBD, RC, CC), F32),
        vm((NBD, RC, CC), F32),
        vm((BS, 2, H * RC + H * 4, CC), F32),
        vm((NR * 4, CC), jnp.int32),
        vm((BS, 2, H, RC, CC), F32),
        vm((NR + 2, RC, CC), F32),
        vm((NR, RC, CC), F32),
        vm((KP, CC), F32),
        vm((KP, CC), F32),
        vm((NR, CC), jnp.int32),
        vm((NR, CC), jnp.int32),
        vm((NR, KP), F32),
        vm((NR, KP), F32),
        dma((7,)), dma((2,)), dma((2 * S,)), dma((2 * S,)), dma((2 * S,)), dma((2 * S,)),
        dma((2,)), dma((2,)), dma((BS,)), dma((BS,)), dma((BS,)), dma((BS,)), dma((BS,)), dma((BS,)), dma((2,)), dma((2,)),
    ]
    need = (10 * L * NBD + 7 * NR) * RC * CC * 4 + 4 * NR * KP * 4 + (8 << 20)
    vmem = pl.BlockSpec(memory_space=pltpu.VMEM)
    hbm = pl.BlockSpec(memory_space=pltpu.HBM)
    shapes = (
        jax.ShapeDtypeStruct(tracers.shape, F32),
        jax.ShapeDtypeStruct((L, NBD, RC, CC), F32),
        jax.ShapeDtypeStruct((slots, RC, CC), F32),
    )
    results = pl.pallas_call(
        functools.partial(kernel, B, S, (L, NBD, RC, CC)),
        out_shape=shapes,
        in_specs=[hbm] * 7,
        out_specs=(vmem,) * 3,
        scratch_shapes=scratch,
        compiler_params=pltpu.CompilerParams(
            collective_id=0, has_side_effects=True, vmem_limit_bytes=need
        ),
    )(*[
        pltpu.with_memory_space_constraint(x, pltpu.HBM)
        for x in (
            tracers, horizontal_diffusivity, vertical_mixing, layer_thickness, surface_diagonal,
            neighbours, baro_blocks,
        )
    ])
    return pl.pallas_call(
        write_out,
        out_shape=shapes,
        in_specs=[vmem] * 3,
        out_specs=(hbm,) * 3,
        scratch_shapes=[dma((4,))],
        compiler_params=pltpu.CompilerParams(vmem_limit_bytes=8 << 20),
    )(*results)


def write_out(tr, p, s, out_tr, out_p, out_s, sem):
    copies = [
        pltpu.make_async_copy(tr.at[0], out_tr.at[0], sem.at[0]),
        pltpu.make_async_copy(tr.at[1], out_tr.at[1], sem.at[1]),
        pltpu.make_async_copy(p, out_p, sem.at[2]),
        pltpu.make_async_copy(s, out_s, sem.at[3]),
    ]
    for copy in copies:
        copy.start()
    for copy in copies:
        copy.wait()


def solution(mesh):
    placed = (
        P("grp", "lev", ("blk", "sub"), None, None),
        P(("blk", "sub"), None, None),
        P(),
        P(),
        P(("blk", "sub"), None, None),
        P(("blk", "sub"), None),
        P(("blk", "sub", "lev")),
    )
    return jax.shard_map(
        local,
        mesh=mesh,
        in_specs=placed,
        out_specs=(
            P("grp", "lev", ("blk", "sub"), None, None),
            P(("grp", "lev"), ("blk", "sub"), None, None),
            P(("grp", "blk", "sub", "lev"), None, None),
        ),
        check_vma=False,
    )
```
